32 devices in a mesh: row: 4 (over x, core), col: 8 (over z, y).
Axes of the slice: x: 2, y: 2, z: 4, core: 2. Of those that a mesh axis runs over, the one named last changes fastest.
Arguments:
- covariance: float32 [8192, 8192], P('row', 'col'), may hold values from -8 to 8, as said below
- couplings: float32 [64, 9, 128, 128], P('row'), may hold values from -0.1875 to 0.1875
- block_columns: int32 [64, 9], replicated, may hold values from 0 to 63, as said below
- onsite: float32 [64], replicated, may hold values from 0.04 to 0.2
Outputs:
- new_covariance: float32 [8192, 8192], P('row', 'col')
The draws below stay inside these ranges and needn't reach their ends.
Inputs may be any that keep to these rules, and one draw needn't show every extreme that they name: `block_columns`: each block row's 9 block columns are distinct and lie within 5 blocks of the row, counted cyclically over the 64 blocks; every row has one block column at distance 5 on each side. The covariance is skew-symmetric.
All inputs are finite; a program needn't handle non-finite values.
Results may differ from the reference program's by a relative error of at most 0.0001.
Values sent between devices are 32-bit elements; how exact they have to be, the bound alone decides.
No kernel may reach another device: no remote copies, remote signals or barrier semaphores. Data moves between devices by JAX's collectives and lax.ppermute only.
A program may use at most 256 MiB of HBM per device.

```python
import math
import jax
import jax.numpy as jnp
from jax import lax

N = 8192
BLOCK = 128
NNZ = 9
REACH = 5
ITERS = 1
NB = 64


def draw_covariance(key, part):
    base = jax.random.normal(key, (N, N), jnp.float32)
    return ((base - base.T) * 0.70710677).astype(jnp.float32)


def draw_block_columns(key, part):
    interior = 2 * REACH - 1
    scores = jax.random.randint(key, (NB, interior), 0, 2 ** 20, dtype=jnp.int32) * interior
    scores = scores + jnp.arange(interior, dtype=jnp.int32)[None, :]
    ordering = jnp.argsort(scores, axis=1, stable=True).astype(jnp.int32)
    picked = ordering[:, :NNZ - 2] - (REACH - 1)
    outer_ends = jnp.broadcast_to(jnp.array([-REACH, REACH], dtype=jnp.int32), (NB, 2))
    offsets = jnp.concatenate([outer_ends, picked], axis=1)
    row_numbers = jnp.arange(NB, dtype=jnp.int32)[:, None]
    return ((row_numbers + offsets) % NB).astype(jnp.int32)


def steps_of(key, extent, cuts, low, top_value):
    level = 1.0
    for position, shards_of in cuts:
        draws = jax.random.uniform(jax.random.fold_in(jax.random.fold_in(key, 6), position), (shards_of,), jnp.float32, low / len(cuts), top_value / len(cuts))
        level = level * jnp.repeat(jnp.exp(draws), extent[position] // shards_of).reshape((-1,) + (1,) * (len(extent) - 1 - position))
    return level


def bell_draw(stream_key, shape, scale, reach, cuts=(), held_as=jnp.bfloat16):
    values = jax.random.normal(stream_key, shape, jnp.float32) * scale
    if len(cuts) > 0:
        values = steps_of(stream_key, shape, cuts, -0.22, 0.18) * values
    return jnp.clip(values, min=-reach, max=reach).astype(held_as)


def setup_inputs(seed: int = 0) -> dict:
    streams_of = jax.random.split(jax.random.key(seed), 5)
    return {
        "covariance": draw_covariance(jax.random.fold_in(streams_of[4], 71), 0),
        "couplings": bell_draw(streams_of[1], (NB, NNZ, BLOCK, BLOCK), (NNZ * BLOCK) ** -0.5, 0.1875, ((0, 4),), jnp.float32),
        "block_columns": draw_block_columns(jax.random.fold_in(streams_of[4], 71), 0),
        "onsite": jnp.clip(jnp.exp(jax.random.uniform(streams_of[3], (NB,), jnp.float32, math.log(0.04), math.log(0.2))), 0.04, 0.2),
    }


step_size = 0.25


def tendency(matrix, couplings, block_columns, onsite):
    positions = jnp.arange(NB, dtype=jnp.int32)
    shaped = matrix.reshape(NB, BLOCK, NB, BLOCK)
    diagonal = shaped[positions, :, positions, :] * onsite[:, None, None]
    row_blocks = matrix.reshape(NB, BLOCK, N)
    col_blocks = jnp.transpose(matrix.reshape(N, NB, BLOCK), (1, 0, 2))

    def row_product(block_row):
        picked = row_blocks[block_columns[block_row]]
        terms = jnp.einsum("kab,kbn->an", couplings[block_row], picked, precision=lax.Precision.HIGHEST)
        return terms + jnp.einsum("ab,bn->an", diagonal[block_row], row_blocks[block_row], precision=lax.Precision.HIGHEST)

    def col_product(block_row):
        picked = col_blocks[block_columns[block_row]]
        terms = jnp.einsum("knb,kab->na", picked, couplings[block_row], precision=lax.Precision.HIGHEST)
        return terms + jnp.einsum("nb,ab->na", col_blocks[block_row], diagonal[block_row], precision=lax.Precision.HIGHEST)

    left_part = lax.map(row_product, positions).reshape(N, N)
    right_part = jnp.transpose(lax.map(col_product, positions), (1, 0, 2)).reshape(N, N)
    return left_part + right_part


def reference(covariance, couplings, block_columns, onsite):
    current = covariance
    for iteration in range(ITERS):
        middle = 0.5 * (covariance + current)
        current = covariance + step_size * tendency(middle, couplings, block_columns, onsite)
    return current
```

```python
import functools

import jax
import jax.numpy as jnp
from jax import lax
from jax.experimental import pallas as pl
from jax.experimental.pallas import tpu as pltpu
from jax.sharding import PartitionSpec as P

BLOCK = 128
REACH = 5


step_size = 0.25


def from_root(block, axis, holder):
    block = jnp.where(lax.axis_index(axis) == holder, block, jnp.zeros_like(block))
    return lax.psum(block, axis)


def shifted(block, axis, distance):
    devices = range(lax.axis_size(axis))
    route = [((i - distance) % len(devices), i) for i in devices]
    return lax.ppermute(block, axis, route)


def relative_positions(columns, first_block, count, total_blocks):
    own_ids = first_block + jnp.arange(count, dtype=jnp.int32)
    relative = (columns - own_ids[:, None] + total_blocks // 2) % total_blocks - total_blocks // 2
    return jnp.arange(count, dtype=jnp.int32)[:, None] + relative + REACH


def general_step(covariance, couplings, block_columns, onsite):
    tile_rows, tile_cols = covariance.shape
    row_blocks = tile_rows // BLOCK
    col_blocks = tile_cols // BLOCK
    total_blocks = block_columns.shape[0]
    reach_cells = REACH * BLOCK
    row_hops = -(-reach_cells // tile_rows)
    col_hops = -(-reach_cells // tile_cols)
    first_row = lax.axis_index("row") * row_blocks
    first_col = lax.axis_index("col") * col_blocks
    own_offset = jnp.clip(first_col - first_row, 0, row_blocks - col_blocks)
    col_root = first_col // row_blocks
    own_couplings = lax.dynamic_slice_in_dim(couplings, own_offset, col_blocks, 0)
    col_couplings = from_root(own_couplings, "row", col_root)
    row_columns = lax.dynamic_slice_in_dim(block_columns, first_row, row_blocks, 0)
    col_columns = lax.dynamic_slice_in_dim(block_columns, first_col, col_blocks, 0)
    row_positions = relative_positions(row_columns, first_row, row_blocks, total_blocks)
    col_positions = relative_positions(col_columns, first_col, col_blocks, total_blocks)
    row_gains = lax.dynamic_slice_in_dim(onsite, first_row, row_blocks, 0)
    col_gains = lax.dynamic_slice_in_dim(onsite, first_col, col_blocks, 0)
    middle = covariance
    shaped = middle.reshape(row_blocks, BLOCK, col_blocks, BLOCK)
    picked = lax.dynamic_slice_in_dim(shaped, own_offset, col_blocks, 0)
    indices = jnp.arange(col_blocks, dtype=jnp.int32)
    local_diagonal = picked[indices, :, indices, :]
    received = []
    for root_part in range(row_blocks // col_blocks):
        received.append(from_root(local_diagonal, "col", first_row // col_blocks + root_part))
    row_diagonal = jnp.concatenate(received, axis=0)
    lower_parts = []
    upper_parts = []
    for distance in range(1, row_hops + 1):
        needed = min(tile_rows, reach_cells - (distance - 1) * tile_rows)
        to_upper = middle[tile_rows - needed :]
        to_lower = middle[:needed]
        from_lower = shifted(to_upper, "row", distance)
        from_upper = shifted(to_lower, "row", -distance)
        lower_parts.insert(0, from_lower)
        upper_parts.append(from_upper)
    extended_rows = jnp.concatenate(lower_parts + [middle] + upper_parts, axis=0).reshape(
        -1, BLOCK, tile_cols
    )
    picked_rows = jnp.take(extended_rows, row_positions, axis=0)
    left_part = jnp.einsum(
        "ikab,ikbn->ian", couplings, picked_rows, precision=lax.Precision.HIGHEST
    )
    left_part = left_part + jnp.einsum(
        "iab,ibn->ian",
        row_diagonal * row_gains[:, None, None],
        middle.reshape(row_blocks, BLOCK, tile_cols),
        precision=lax.Precision.HIGHEST,
    )
    left_part = left_part.reshape(tile_rows, tile_cols)
    col_diagonal = from_root(local_diagonal, "row", col_root)
    left_parts = []
    right_parts = []
    for distance in range(1, col_hops + 1):
        needed = min(tile_cols, reach_cells - (distance - 1) * tile_cols)
        to_right = middle[:, tile_cols - needed :]
        to_left = middle[:, :needed]
        from_left = shifted(to_right, "col", distance)
        from_right = shifted(to_left, "col", -distance)
        left_parts.insert(0, from_left)
        right_parts.append(from_right)
    extended_cols = jnp.concatenate(left_parts + [middle] + right_parts, axis=1).reshape(
        tile_rows, -1, BLOCK
    )
    picked_cols = jnp.take(extended_cols, col_positions, axis=1)
    right_part = jnp.einsum(
        "nikb,ikab->nia", picked_cols, col_couplings, precision=lax.Precision.HIGHEST
    )
    right_part = right_part + jnp.einsum(
        "nib,iab->nia",
        middle.reshape(tile_rows, col_blocks, BLOCK),
        col_diagonal * col_gains[:, None, None],
        precision=lax.Precision.HIGHEST,
    )
    right_part = right_part.reshape(tile_rows, tile_cols)
    return covariance + step_size * (left_part + right_part)


GROUP = 2
WINDOW = (GROUP + 2 * REACH) * BLOCK
HALO = REACH * BLOCK
VMEM = 56 * 1024 * 1024


def halves(value):
    high = value.astype(jnp.bfloat16)
    return high, (value - high.astype(jnp.float32)).astype(jnp.bfloat16)


def product(a_high, a_low, b_high, b_low, contract_b=0):
    dims = (((1,), (contract_b,)), ((), ()))
    dot = functools.partial(lax.dot_general, dimension_numbers=dims, preferred_element_type=jnp.float32)
    return dot(a_high, b_high) + (dot(a_high, b_low) + dot(a_low, b_high))


def band_kernel(places, gains, blocks, diagonal, high, low, whole, *, with_diagonal):
    i = pl.program_id(0)
    whole[...] = jnp.zeros_like(whole)
    for k in range(blocks.shape[1]):
        place = pl.multiple_of(places[i, k] * BLOCK, BLOCK)
        whole[:, pl.ds(place, BLOCK)] = blocks[0, k]
    if with_diagonal:
        own = pl.multiple_of((REACH + i % GROUP) * BLOCK, BLOCK)
        whole[:, pl.ds(own, BLOCK)] += gains[i] * diagonal[0]
    high[...], low[...] = halves(whole[...])


def band(blocks, columns, first_block, total_blocks, diagonal, gains):
    count, stored = columns.shape
    own_ids = first_block + jnp.arange(count, dtype=jnp.int32)
    relative = (columns - own_ids[:, None] + total_blocks // 2) % total_blocks - total_blocks // 2
    places = relative + REACH + (jnp.arange(count, dtype=jnp.int32) % GROUP)[:, None]
    with_diagonal = diagonal is not None
    if not with_diagonal:
        diagonal = jnp.zeros((1, BLOCK, BLOCK), jnp.float32)
    shape = jax.ShapeDtypeStruct((count * BLOCK, WINDOW), jnp.bfloat16)
    return pl.pallas_call(
        functools.partial(band_kernel, with_diagonal=with_diagonal),
        out_shape=(shape, shape),
        grid_spec=pltpu.PrefetchScalarGridSpec(
            num_scalar_prefetch=2,
            grid=(count,),
            in_specs=[
                pl.BlockSpec((1, stored, BLOCK, BLOCK), lambda i, *_: (i, 0, 0, 0)),
                pl.BlockSpec((1, BLOCK, BLOCK), lambda i, *_: (i if with_diagonal else 0, 0, 0)),
            ],
            out_specs=[pl.BlockSpec((BLOCK, WINDOW), lambda i, *_: (i, 0))] * 2,
            scratch_shapes=[pltpu.VMEM((BLOCK, WINDOW), jnp.float32)],
        ),
        compiler_params=pltpu.CompilerParams(vmem_limit_bytes=VMEM),
        cost_estimate=pl.CostEstimate(
            flops=0, bytes_accessed=count * BLOCK * (stored * BLOCK + WINDOW) * 4, transcendentals=0
        ),
        name="band",
    )(places, gains, blocks, diagonal)


def left_kernel(top, own, bottom, high, low, out, ext_high, ext_low):
    rows = own.shape[0]
    for start, part in ((0, top), (HALO, own), (HALO + rows, bottom)):
        size = part.shape[0]
        ext_high[start : start + size], ext_low[start : start + size] = halves(part[...])
    step = GROUP * BLOCK
    for g in range(rows // step):
        here, window = slice(g * step, (g + 1) * step), slice(g * step, g * step + WINDOW)
        value = product(high[here], low[here], ext_high[window], ext_low[window])
        out[here] = own[here] + step_size * value


def left_part(top, covariance, bottom, high, low, slab=256):
    rows, cols = covariance.shape
    whole = pl.BlockSpec((rows, WINDOW), lambda j: (0, 0), pipeline_mode=pl.Buffered(1))
    return pl.pallas_call(
        left_kernel,
        out_shape=jax.ShapeDtypeStruct((rows, cols), jnp.float32),
        grid=(cols // slab,),
        in_specs=[
            pl.BlockSpec((HALO, slab), lambda j: (0, j)),
            pl.BlockSpec((rows, slab), lambda j: (0, j)),
            pl.BlockSpec((HALO, slab), lambda j: (0, j)),
            whole,
            whole,
        ],
        out_specs=pl.BlockSpec((rows, slab), lambda j: (0, j)),
        scratch_shapes=[pltpu.VMEM((rows + 2 * HALO, slab), jnp.bfloat16)] * 2,
        compiler_params=pltpu.CompilerParams(vmem_limit_bytes=VMEM),
        cost_estimate=pl.CostEstimate(
            flops=6 * rows * cols * WINDOW, bytes_accessed=12 * rows * cols, transcendentals=0
        ),
        name="left_part",
    )(top, covariance, bottom, high, low)


def right_kernel(odd, pair, strip, own, row_diagonal, high, low, total, out, ext_high, ext_low):
    rows, cols = own.shape

    def put(start, value):
        end = start + value.shape[1]
        ext_high[:, start:end], ext_low[:, start:end] = halves(value)

    put(HALO, own[...])

    @pl.when(odd[0] == 0)
    def _():
        put(0, strip[...])
        put(HALO + cols, pair[:, :HALO])

    @pl.when(odd[0] == 1)
    def _():
        put(0, pair[:, cols - HALO :])
        put(HALO + cols, strip[...])

    step = GROUP * BLOCK
    for g in range(cols // step):
        here, window = slice(g * step, (g + 1) * step), slice(g * step, g * step + WINDOW)
        value = product(ext_high[:, window], ext_low[:, window], high[here], low[here], 1)
        out[:, here] = total[:, here] + step_size * value
    for b in range(rows // BLOCK):
        here, mine = slice(b * BLOCK, (b + 1) * BLOCK), slice(HALO, HALO + cols)
        onsite_high, onsite_low = halves(row_diagonal[b])
        value = product(onsite_high, onsite_low, ext_high[here, mine], ext_low[here, mine])
        out[here] += step_size * value


def right_part(first, odd, pair, strip, covariance, row_diagonal, high, low, total, rows):
    cols = covariance.shape[1]
    count = pair.shape[0] // rows
    scalars = jnp.stack([odd, first // rows]).astype(jnp.int32)
    whole = pl.BlockSpec(high.shape, lambda j, s: (0, 0), pipeline_mode=pl.Buffered(1))
    there = pl.BlockSpec((rows, cols), lambda j, s: (s[1] + j, 0))
    return pl.pallas_call(
        right_kernel,
        out_shape=jax.ShapeDtypeStruct(total.shape, jnp.float32),
        grid_spec=pltpu.PrefetchScalarGridSpec(
            num_scalar_prefetch=1,
            grid=(count,),
            in_specs=[
                pl.BlockSpec((rows, cols), lambda j, s: (j, 0)),
                pl.BlockSpec((rows, HALO), lambda j, s: (j, 0)),
                there,
                pl.BlockSpec((rows // BLOCK, BLOCK, BLOCK), lambda j, s: (s[1] + j, 0, 0)),
                whole,
                whole,
                there,
            ],
            out_specs=there,
            scratch_shapes=[pltpu.VMEM((rows, cols + 2 * HALO), jnp.bfloat16)] * 2,
        ),
        input_output_aliases={7: 0},
        compiler_params=pltpu.CompilerParams(vmem_limit_bytes=VMEM),
        cost_estimate=pl.CostEstimate(
            flops=6 * rows * count * cols * WINDOW, bytes_accessed=18 * rows * count * cols, transcendentals=0
        ),
        name="right_part",
    )(scalars, pair, strip, covariance, row_diagonal, high, low, total)


def send(value, pairs, cols):
    return lax.ppermute(value, ("row", "col"), [(a * cols + b, c * cols + d) for (a, b), (c, d) in pairs])


def spread_over_rows(value, mesh_rows, mesh_cols, ratio):
    place = lax.axis_index("row") ^ (lax.axis_index("col") // ratio)
    hop = mesh_rows // 2
    while hop:
        pairs = []
        for r in range(mesh_rows):
            for c in range(mesh_cols):
                if (r ^ (c // ratio)) & (2 * hop - 1) == 0:
                    pairs.append(((r, c), (r ^ hop, c)))
        value = jnp.where(place & (2 * hop - 1) == hop, send(value, pairs, mesh_cols), value)
        hop //= 2
    return value


def spread_over_cols(value, mesh_rows, mesh_cols, ratio):
    place = (lax.axis_index("col") // ratio) ^ lax.axis_index("row")
    hop = mesh_cols // ratio // 2
    while hop:
        pairs = []
        for r in range(mesh_rows):
            for c in range(mesh_cols):
                if ((c // ratio) ^ r) & (2 * hop - 1) == 0:
                    pairs.append(((r, c), (r, ((c // ratio) ^ hop) * ratio + c % ratio)))
        value = jnp.where(place & (2 * hop - 1) == hop, send(value, pairs, mesh_cols), value)
        hop //= 2
    return value


def cut(total):
    sizes = []
    left = total
    while left:
        size = max(BLOCK, (left // 4) // (2 * BLOCK) * 2 * BLOCK)
        sizes.append(min(size, left))
        left -= sizes[-1]
    return sizes


def paired_step(covariance, couplings, block_columns, onsite):
    tile_rows, tile_cols = covariance.shape
    row_blocks, col_blocks = tile_rows // BLOCK, tile_cols // BLOCK
    total_blocks = block_columns.shape[0]
    mesh_rows, mesh_cols = lax.axis_size("row"), lax.axis_size("col")
    ratio = tile_rows // tile_cols
    row, col = lax.axis_index("row"), lax.axis_index("col")
    odd = col % 2
    first_row, first_col = row * row_blocks, col * col_blocks
    offset = jnp.clip(first_col - first_row, 0, row_blocks - col_blocks)
    devices = [(r, c) for r in range(mesh_rows) for c in range(mesh_cols)]

    top = shifted(covariance[tile_rows - HALO :], "row", 1)
    bottom = shifted(covariance[:HALO], "row", -1)

    diagonal = jnp.stack(
        [
            lax.dynamic_slice(covariance, ((offset + j) * BLOCK, j * BLOCK), (BLOCK, BLOCK))
            for j in range(col_blocks)
        ]
    )
    other = send(diagonal, [((r, c), (r, c ^ 1)) for r, c in devices if c // 2 == r], mesh_cols)
    both = jnp.where(odd == 0, jnp.stack([diagonal, other]), jnp.stack([other, diagonal]))
    row_diagonal = spread_over_cols(both.reshape(row_blocks, BLOCK, BLOCK), mesh_rows, mesh_cols, ratio)
    row_gains = lax.dynamic_slice_in_dim(onsite, first_row, row_blocks, 0)
    row_diagonal = row_diagonal * row_gains[:, None, None]

    own_couplings = lax.dynamic_slice_in_dim(couplings, offset, col_blocks, 0)
    col_couplings = spread_over_rows(own_couplings, mesh_rows, mesh_cols, ratio)
    col_diagonal = spread_over_rows(diagonal, mesh_rows, mesh_cols, ratio)

    pairs, strips, firsts = [], [], []
    start = 0
    for size in cut(tile_rows):
        chunk = covariance[start : start + size]
        pair = send(chunk, [((r, c), (r, c ^ 1)) for r, c in devices], mesh_cols)
        strip = lax.dynamic_slice_in_dim(pair, (1 - odd) * (tile_cols - HALO), HALO, 1)
        strip = send(
            strip, [((r, c), (r, (c + (2 if c % 2 == 0 else -2)) % mesh_cols)) for r, c in devices], mesh_cols
        )
        pairs.append(pair)
        strips.append(strip)
        firsts.append(start)
        start += size

    row_columns = lax.dynamic_slice_in_dim(block_columns, first_row, row_blocks, 0)
    row_high, row_low = band(couplings, row_columns, first_row, total_blocks, None, row_gains)
    total = left_part(top, covariance, bottom, row_high, row_low)

    col_columns = lax.dynamic_slice_in_dim(block_columns, first_col, col_blocks, 0)
    col_gains = lax.dynamic_slice_in_dim(onsite, first_col, col_blocks, 0)
    col_high, col_low = band(col_couplings, col_columns, first_col, total_blocks, col_diagonal, col_gains)
    for first, pair, strip in zip(firsts, pairs, strips):
        rows = 2 * BLOCK if pair.shape[0] % (2 * BLOCK) == 0 and first % (2 * BLOCK) == 0 else BLOCK
        total = right_part(
            jnp.int32(first), odd, pair, strip, covariance, row_diagonal, col_high, col_low, total, rows
        )
    return total


def power_of_two(number):
    return number & (number - 1) == 0


def on_device(covariance, couplings, block_columns, onsite):
    tile_rows, tile_cols = covariance.shape
    mesh_rows, mesh_cols = lax.axis_size("row"), lax.axis_size("col")
    fits = (
        tile_cols >= HALO
        and tile_cols % (GROUP * BLOCK) == 0
        and tile_rows == 2 * tile_cols
        and mesh_cols == 2 * mesh_rows
        and power_of_two(mesh_rows)
        and block_columns.shape[0] >= 2 * REACH + 2
    )
    step = paired_step if fits else general_step
    return step(covariance, couplings, block_columns, onsite)


def solution(mesh):
    return jax.shard_map(
        on_device,
        mesh=mesh,
        in_specs=(P("row", "col"), P("row", None, None, None), P(), P()),
        out_specs=P("row", "col"),
        check_vma=False,
    )
```

```python
import functools

import jax
import jax.numpy as jnp
from jax import lax
from jax.experimental import pallas as pl
from jax.experimental.pallas import tpu as pltpu
from jax.sharding import PartitionSpec as P

BLOCK = 128
REACH = 5


step_size = 0.25


def from_root(block, axis, holder):
    block = jnp.where(lax.axis_index(axis) == holder, block, jnp.zeros_like(block))
    return lax.psum(block, axis)


def shifted(block, axis, distance):
    devices = range(lax.axis_size(axis))
    route = [((i - distance) % len(devices), i) for i in devices]
    return lax.ppermute(block, axis, route)


def relative_positions(columns, first_block, count, total_blocks):
    own_ids = first_block + jnp.arange(count, dtype=jnp.int32)
    relative = (columns - own_ids[:, None] + total_blocks // 2) % total_blocks - total_blocks // 2
    return jnp.arange(count, dtype=jnp.int32)[:, None] + relative + REACH


def general_step(covariance, couplings, block_columns, onsite):
    tile_rows, tile_cols = covariance.shape
    row_blocks = tile_rows // BLOCK
    col_blocks = tile_cols // BLOCK
    total_blocks = block_columns.shape[0]
    reach_cells = REACH * BLOCK
    row_hops = -(-reach_cells // tile_rows)
    col_hops = -(-reach_cells // tile_cols)
    first_row = lax.axis_index("row") * row_blocks
    first_col = lax.axis_index("col") * col_blocks
    own_offset = jnp.clip(first_col - first_row, 0, row_blocks - col_blocks)
    col_root = first_col // row_blocks
    own_couplings = lax.dynamic_slice_in_dim(couplings, own_offset, col_blocks, 0)
    col_couplings = from_root(own_couplings, "row", col_root)
    row_columns = lax.dynamic_slice_in_dim(block_columns, first_row, row_blocks, 0)
    col_columns = lax.dynamic_slice_in_dim(block_columns, first_col, col_blocks, 0)
    row_positions = relative_positions(row_columns, first_row, row_blocks, total_blocks)
    col_positions = relative_positions(col_columns, first_col, col_blocks, total_blocks)
    row_gains = lax.dynamic_slice_in_dim(onsite, first_row, row_blocks, 0)
    col_gains = lax.dynamic_slice_in_dim(onsite, first_col, col_blocks, 0)
    middle = covariance
    shaped = middle.reshape(row_blocks, BLOCK, col_blocks, BLOCK)
    picked = lax.dynamic_slice_in_dim(shaped, own_offset, col_blocks, 0)
    indices = jnp.arange(col_blocks, dtype=jnp.int32)
    local_diagonal = picked[indices, :, indices, :]
    received = []
    for root_part in range(row_blocks // col_blocks):
        received.append(from_root(local_diagonal, "col", first_row // col_blocks + root_part))
    row_diagonal = jnp.concatenate(received, axis=0)
    lower_parts = []
    upper_parts = []
    for distance in range(1, row_hops + 1):
        needed = min(tile_rows, reach_cells - (distance - 1) * tile_rows)
        to_upper = middle[tile_rows - needed :]
        to_lower = middle[:needed]
        from_lower = shifted(to_upper, "row", distance)
        from_upper = shifted(to_lower, "row", -distance)
        lower_parts.insert(0, from_lower)
        upper_parts.append(from_upper)
    extended_rows = jnp.concatenate(lower_parts + [middle] + upper_parts, axis=0).reshape(
        -1, BLOCK, tile_cols
    )
    picked_rows = jnp.take(extended_rows, row_positions, axis=0)
    left_part = jnp.einsum(
        "ikab,ikbn->ian", couplings, picked_rows, precision=lax.Precision.HIGHEST
    )
    left_part = left_part + jnp.einsum(
        "iab,ibn->ian",
        row_diagonal * row_gains[:, None, None],
        middle.reshape(row_blocks, BLOCK, tile_cols),
        precision=lax.Precision.HIGHEST,
    )
    left_part = left_part.reshape(tile_rows, tile_cols)
    col_diagonal = from_root(local_diagonal, "row", col_root)
    left_parts = []
    right_parts = []
    for distance in range(1, col_hops + 1):
        needed = min(tile_cols, reach_cells - (distance - 1) * tile_cols)
        to_right = middle[:, tile_cols - needed :]
        to_left = middle[:, :needed]
        from_left = shifted(to_right, "col", distance)
        from_right = shifted(to_left, "col", -distance)
        left_parts.insert(0, from_left)
        right_parts.append(from_right)
    extended_cols = jnp.concatenate(left_parts + [middle] + right_parts, axis=1).reshape(
        tile_rows, -1, BLOCK
    )
    picked_cols = jnp.take(extended_cols, col_positions, axis=1)
    right_part = jnp.einsum(
        "nikb,ikab->nia", picked_cols, col_couplings, precision=lax.Precision.HIGHEST
    )
    right_part = right_part + jnp.einsum(
        "nib,iab->nia",
        middle.reshape(tile_rows, col_blocks, BLOCK),
        col_diagonal * col_gains[:, None, None],
        precision=lax.Precision.HIGHEST,
    )
    right_part = right_part.reshape(tile_rows, tile_cols)
    return covariance + step_size * (left_part + right_part)


GROUP = 2
WINDOW = (GROUP + 2 * REACH) * BLOCK
HALO = REACH * BLOCK
VMEM = 56 * 1024 * 1024
SHORT = pl.CostEstimate(flops=1, bytes_accessed=1, transcendentals=0)
TOKEN = jax.ShapeDtypeStruct((8, 128), jnp.float32)
TOKEN_SPEC = pl.BlockSpec((8, 128), lambda *_: (0, 0))


def halves(value):
    high = value.astype(jnp.bfloat16)
    return high, (value - high.astype(jnp.float32)).astype(jnp.bfloat16)


def product(a_high, a_low, b_high, b_low, contract_b=0):
    dims = (((1,), (contract_b,)), ((), ()))
    dot = functools.partial(lax.dot_general, dimension_numbers=dims, preferred_element_type=jnp.float32)
    return dot(a_high, b_high) + (dot(a_high, b_low) + dot(a_low, b_high))


def band_kernel(places, gains, choice, *refs, sources, with_diagonal):
    blocks, diagonal, (high, low, token, whole) = refs[:sources], refs[sources], refs[sources + 1 :]
    token[...] = jnp.zeros_like(token)
    i = pl.program_id(0)
    whole[...] = jnp.zeros_like(whole)
    for source in range(sources):

        @pl.when(choice[0] == source)
        def _():
            for k in range(blocks[source].shape[0]):
                place = pl.multiple_of(places[i, k] * BLOCK, BLOCK)
                whole[:, pl.ds(place, BLOCK)] = blocks[source][k]

    if with_diagonal:
        own = pl.multiple_of((REACH + i % GROUP) * BLOCK, BLOCK)
        whole[:, pl.ds(own, BLOCK)] += gains[i] * diagonal[0]
    high[...], low[...] = halves(whole[...])


def band(sources, choice, offset, columns, first_block, total_blocks, diagonal, gains):
    count, stored = columns.shape
    own_ids = first_block + jnp.arange(count, dtype=jnp.int32)
    relative = (columns - own_ids[:, None] + total_blocks // 2) % total_blocks - total_blocks // 2
    places = relative + REACH + (jnp.arange(count, dtype=jnp.int32) % GROUP)[:, None]
    with_diagonal = diagonal is not None
    if not with_diagonal:
        diagonal = jnp.zeros((1, BLOCK, BLOCK), jnp.float32)
    shape = jax.ShapeDtypeStruct((count * BLOCK, WINDOW), jnp.bfloat16)

    def blocks_of(source):
        def index(i, places, gains, choice):
            start = choice[1] if source == 0 else 0
            return (jnp.where(choice[0] == source, start + i, 0), 0, 0)

        return pl.BlockSpec((stored, BLOCK, BLOCK), index)

    return pl.pallas_call(
        functools.partial(band_kernel, sources=len(sources), with_diagonal=with_diagonal),
        out_shape=(shape, shape, TOKEN),
        grid_spec=pltpu.PrefetchScalarGridSpec(
            num_scalar_prefetch=3,
            grid=(count,),
            in_specs=[
                *(blocks_of(source) for source in range(len(sources))),
                pl.BlockSpec((1, BLOCK, BLOCK), lambda i, *_: (i if with_diagonal else 0, 0, 0)),
            ],
            out_specs=[pl.BlockSpec((BLOCK, WINDOW), lambda i, *_: (i, 0))] * 2 + [TOKEN_SPEC],
            scratch_shapes=[pltpu.VMEM((BLOCK, WINDOW), jnp.float32)],
        ),
        compiler_params=pltpu.CompilerParams(vmem_limit_bytes=VMEM),
        cost_estimate=SHORT,
        name="band",
    )(places, gains, jnp.stack([choice, offset]).astype(jnp.int32), *sources, diagonal)


def left_kernel(up, inner, own, outer, high, low, out, token, ext_high, ext_low):
    token[...] = jnp.zeros_like(token)
    rows = own.shape[0]
    top = jnp.where(up[0] == 0, outer[...], inner[...])
    bottom = jnp.where(up[0] == 0, inner[...], outer[...])
    for start, part in ((0, top), (HALO, own[...]), (HALO + rows, bottom)):
        size = part.shape[0]
        ext_high[start : start + size], ext_low[start : start + size] = halves(part)
    step = GROUP * BLOCK
    for g in range(rows // step):
        here, window = slice(g * step, (g + 1) * step), slice(g * step, g * step + WINDOW)
        value = product(high[here], low[here], ext_high[window], ext_low[window])
        out[here] = own[here] + step_size * value


def left_part(up, inner, covariance, outer, high, low, slab=256):
    rows, cols = covariance.shape
    whole = pl.BlockSpec((rows, WINDOW), lambda j, s: (0, 0), pipeline_mode=pl.Buffered(1))
    beyond = pl.BlockSpec((HALO, slab), lambda j, s: (0, j))
    here = pl.BlockSpec((rows, slab), lambda j, s: (0, j))
    return pl.pallas_call(
        left_kernel,
        out_shape=(jax.ShapeDtypeStruct((rows, cols), jnp.float32), TOKEN),
        grid_spec=pltpu.PrefetchScalarGridSpec(
            num_scalar_prefetch=1,
            grid=(cols // slab,),
            in_specs=[beyond, here, beyond, whole, whole],
            out_specs=[here, TOKEN_SPEC],
            scratch_shapes=[pltpu.VMEM((rows + 2 * HALO, slab), jnp.bfloat16)] * 2,
        ),
        compiler_params=pltpu.CompilerParams(vmem_limit_bytes=VMEM),
        cost_estimate=SHORT,
        name="left_part",
    )(up.reshape(1).astype(jnp.int32), inner, covariance, outer, high, low)


def right_kernel(odd, pair, strip, own, row_diagonal, high, low, total, out, token, ext_high, ext_low):
    token[...] = jnp.zeros_like(token)
    rows, cols = own.shape

    def put(start, value):
        end = start + value.shape[1]
        ext_high[:, start:end], ext_low[:, start:end] = halves(value)

    put(HALO, own[...])

    @pl.when(odd[0] == 0)
    def _():
        put(0, strip[...])
        put(HALO + cols, pair[:, :HALO])

    @pl.when(odd[0] == 1)
    def _():
        put(0, pair[:, cols - HALO :])
        put(HALO + cols, strip[...])

    step = GROUP * BLOCK
    for g in range(cols // step):
        here, window = slice(g * step, (g + 1) * step), slice(g * step, g * step + WINDOW)
        value = product(ext_high[:, window], ext_low[:, window], high[here], low[here], 1)
        out[:, here] = total[:, here] + step_size * value
    for b in range(rows // BLOCK):
        here, mine = slice(b * BLOCK, (b + 1) * BLOCK), slice(HALO, HALO + cols)
        onsite_high, onsite_low = halves(row_diagonal[b])
        value = product(onsite_high, onsite_low, ext_high[here, mine], ext_low[here, mine])
        out[here] += step_size * value


def right_part(first, odd, pair, strip, covariance, row_diagonal, high, low, total, rows):
    cols = covariance.shape[1]
    count = pair.shape[0] // rows
    scalars = jnp.stack([odd, first]).astype(jnp.int32)
    whole = pl.BlockSpec(high.shape, lambda j, s: (0, 0), pipeline_mode=pl.Buffered(1))
    there = pl.BlockSpec((pl.Element(rows), pl.Element(cols)), lambda j, s: (pl.multiple_of(s[1] + j * rows, BLOCK), 0))
    return pl.pallas_call(
        right_kernel,
        out_shape=(jax.ShapeDtypeStruct(total.shape, jnp.float32), TOKEN),
        grid_spec=pltpu.PrefetchScalarGridSpec(
            num_scalar_prefetch=1,
            grid=(count,),
            in_specs=[
                pl.BlockSpec((rows, cols), lambda j, s: (j, 0)),
                pl.BlockSpec((rows, HALO), lambda j, s: (j, 0)),
                there,
                pl.BlockSpec((pl.Element(rows // BLOCK), pl.Element(BLOCK), pl.Element(BLOCK)), lambda j, s: (s[1] // BLOCK + j * (rows // BLOCK), 0, 0)),
                whole,
                whole,
                there,
            ],
            out_specs=[there, TOKEN_SPEC],
            scratch_shapes=[pltpu.VMEM((rows, cols + 2 * HALO), jnp.bfloat16)] * 2,
        ),
        input_output_aliases={7: 0},
        compiler_params=pltpu.CompilerParams(vmem_limit_bytes=VMEM),
        cost_estimate=SHORT,
        name="right_part",
    )(scalars, pair, strip, covariance, row_diagonal, high, low, total)


def send(value, pairs, cols):
    return lax.ppermute(value, ("row", "col"), [(a * cols + b, c * cols + d) for (a, b), (c, d) in pairs])


def rows_route(hop, devices, ratio):
    return [((r, c), (r ^ hop, c)) for r, c in devices if (r ^ (c // ratio)) & (2 * hop - 1) == 0]


def cols_route(hop, devices, ratio):
    return [
        ((r, c), (r, ((c // ratio) ^ hop) * ratio + c % ratio))
        for r, c in devices
        if ((c // ratio) ^ r) & (2 * hop - 1) == 0
    ]


def cut(total):
    first = total * 5 // 16 // BLOCK * BLOCK
    sizes = [first, first]
    left = total - 2 * first
    while left > BLOCK:
        sizes.append(-(-left // (2 * BLOCK)) * BLOCK)
        left -= sizes[-1]
    return sizes + [left] * (left > 0)


def packed_kernel(first, upper, lower, out):
    across = lax.broadcasted_iota(jnp.int32, (BLOCK, BLOCK), 1)
    down = lax.broadcasted_iota(jnp.int32, (BLOCK, BLOCK), 0)
    out[0] = jnp.where(across > down, upper[...], jnp.where(across < down, lower[...], 0.0))


def packed_diagonal(covariance, first, count):
    half = count // 2
    return pl.pallas_call(
        packed_kernel,
        out_shape=jax.ShapeDtypeStruct((half, BLOCK, BLOCK), jnp.float32),
        grid_spec=pltpu.PrefetchScalarGridSpec(
            num_scalar_prefetch=1,
            grid=(half,),
            in_specs=[
                pl.BlockSpec((BLOCK, BLOCK), lambda j, s: (s[0] + j, j)),
                pl.BlockSpec((BLOCK, BLOCK), lambda j, s: (s[0] + half + j, half + j)),
            ],
            out_specs=pl.BlockSpec((1, BLOCK, BLOCK), lambda j, s: (j, 0, 0)),
        ),
        cost_estimate=SHORT,
        name="packed_diagonal",
    )(first.reshape(1).astype(jnp.int32), covariance, covariance)


def unpacked(blocks):
    upper, lower = jnp.triu(blocks), jnp.tril(blocks)
    return jnp.concatenate([upper - upper.transpose(0, 2, 1), lower - lower.transpose(0, 2, 1)], axis=0)


class Order:
    def __init__(self):
        self.clock = jnp.zeros(TOKEN.shape, TOKEN.dtype)

    def after(self, value):
        return lax.optimization_barrier((value, self.clock))[0]

    def passed(self, value):
        value, self.clock = lax.optimization_barrier((value, self.clock))
        return value

    def ran(self, results):
        self.clock = results[-1]
        return results[:-1]


def paired_step(covariance, couplings, block_columns, onsite):
    tile_rows, tile_cols = covariance.shape
    row_blocks, col_blocks = tile_rows // BLOCK, tile_cols // BLOCK
    total_blocks, stored = block_columns.shape
    mesh_rows, mesh_cols = lax.axis_size("row"), lax.axis_size("col")
    ratio = tile_rows // tile_cols
    row, col = lax.axis_index("row"), lax.axis_index("col")
    odd, up = col % 2, row % 2
    first_row, first_col = row * row_blocks, col * col_blocks
    offset = jnp.clip(first_col - first_row, 0, row_blocks - col_blocks)
    devices = [(r, c) for r in range(mesh_rows) for c in range(mesh_cols)]
    partners = [((r, c), (r, c ^ 1)) for r, c in devices]
    next_pairs = [((r, c), (r, (c + (2 if c % 2 == 0 else -2)) % mesh_cols)) for r, c in devices]
    inner_route = [((r, c), (r ^ 1, c)) for r, c in devices]
    outer_route = [((r, c), ((r + (-1 if r % 2 == 0 else 1)) % mesh_rows, c)) for r, c in devices]
    beside = 0
    sizes = cut(tile_rows - beside)
    firsts = [sum(sizes[:j]) for j in range(len(sizes))]
    order = Order()
    chunks, pairs, strips = {}, {}, {}

    def move(value, route):
        return send(order.after(value), route, mesh_cols)

    def prepare(*numbers):
        for j in numbers:
            if j < len(sizes):
                chunk = lax.dynamic_slice_in_dim(covariance, beside * odd + firsts[j], sizes[j], 0)
                chunks[j] = order.passed(chunk)

    def exchange(*numbers):
        for j in numbers:
            if j < len(sizes):
                pairs[j] = move(chunks[j], partners)

    def exchanged(j):
        pairs[j] = order.passed(pairs[j])
        strip = lax.dynamic_slice_in_dim(pairs[j], (1 - odd) * (tile_cols - HALO), HALO, 1)
        strips[j] = move(strip, next_pairs)

    def add_right(total, j):
        first = beside * (1 - odd) + firsts[j]
        (total,) = order.ran(
            right_part(
                order.after(jnp.int32(first)), odd, pairs[j], strips[j], covariance, row_diagonal,
                col_high, col_low, total, sizes[j],
            )
        )
        return total

    far = tile_rows - HALO
    diagonal = packed_diagonal(covariance, offset, col_blocks)
    other = move(diagonal, [((r, c), (r, c ^ 1)) for r, c in devices if c // 2 == r])
    prepare(0)
    exchange(0)
    outer = move(lax.dynamic_slice_in_dim(covariance, up * far, HALO, 0), outer_route)
    inner = move(lax.dynamic_slice_in_dim(covariance, (1 - up) * far, HALO, 0), inner_route)
    row_gains = lax.dynamic_slice_in_dim(onsite, first_row, row_blocks, 0)
    row_columns = lax.dynamic_slice_in_dim(block_columns, first_row, row_blocks, 0)
    blocks = couplings.reshape(-1, BLOCK, BLOCK)
    zero = jnp.int32(0)
    row_high, row_low = order.ran(
        band([blocks], zero, zero, row_columns, first_row, total_blocks, None, order.after(row_gains))
    )
    count = col_blocks * stored
    own_blocks = lax.dynamic_slice_in_dim(blocks, offset * stored, count, 0)
    held = {0: order.passed(jnp.concatenate([own_blocks, diagonal], axis=0))}
    prepare(1)
    inner, outer, other = order.passed(inner), order.passed(outer), order.passed(other)

    def hand_on(place):
        low = place & -place
        route = [((r, c), (r ^ low, c)) for r, c in devices if r ^ (c // ratio) == place ^ low]
        held[place] = move(held[place ^ low], route)

    exchanged(0)
    exchange(1)
    places = sorted(range(1, mesh_rows), key=lambda place: (bin(place).count("1"), -place))
    nearest = [place for place in places if place & (place - 1) == 0]
    for place in nearest:
        hand_on(place)
    both = jnp.where(odd == 0, jnp.stack([diagonal, other]), jnp.stack([other, diagonal]))
    both = both.reshape(-1, BLOCK, BLOCK)
    across, hop = (col // ratio) ^ row, mesh_cols // ratio // 2
    moved = move(both, cols_route(hop, devices, ratio))
    (total,) = order.ran(left_part(order.after(up), inner, covariance, outer, row_high, row_low))
    moved = order.passed(moved)
    both = jnp.where(across & (2 * hop - 1) == hop, moved, both)
    while hop > 1:
        hop //= 2
        moved = move(both, cols_route(hop, devices, ratio))
        if hop > 1:
            moved = order.passed(moved)
            both = jnp.where(across & (2 * hop - 1) == hop, moved, both)
    prepare(2, 3)
    strips[0] = order.passed(strips[0])
    for place in nearest:
        held[place] = order.passed(held[place])
    moved = order.passed(moved)
    both = jnp.where(across & 1 == 1, moved, both)
    half = both.shape[0] // 2
    row_diagonal = jnp.concatenate([unpacked(both[:half]), unpacked(both[half:])], axis=0)
    row_diagonal = order.passed(row_diagonal * row_gains[:, None, None])

    exchanged(1)
    exchange(2, 3)
    for place in places[len(nearest) :]:
        hand_on(place)
        held[place] = order.passed(held[place])
    prepare(4, 5)
    place = row ^ (col // ratio)
    col_diagonal = held[0][count:]
    for source in places:
        col_diagonal = jnp.where(place == source, held[source][count:], col_diagonal)
    col_diagonal = unpacked(col_diagonal)
    col_columns = lax.dynamic_slice_in_dim(block_columns, first_col, col_blocks, 0)
    col_gains = lax.dynamic_slice_in_dim(onsite, first_col, col_blocks, 0)
    col_high, col_low = order.ran(
        band(
            [blocks] + [held[source] for source in sorted(places)],
            place, offset, col_columns, first_col, total_blocks, order.after(col_diagonal), col_gains,
        )
    )
    total = add_right(total, 0)
    for j in range(2, len(sizes)):
        exchanged(j)
        exchange(j + 2)
        strips[j - 1] = order.passed(strips[j - 1])
        total = add_right(total, j - 1)
    strips[len(sizes) - 1] = order.passed(strips[len(sizes) - 1])
    return add_right(total, len(sizes) - 1)


def power_of_two(number):
    return number & (number - 1) == 0


def on_device(covariance, couplings, block_columns, onsite):
    tile_rows, tile_cols = covariance.shape
    mesh_rows, mesh_cols = lax.axis_size("row"), lax.axis_size("col")
    fits = (
        tile_cols >= HALO
        and tile_cols % (GROUP * BLOCK) == 0
        and tile_rows == 2 * tile_cols
        and mesh_cols == 2 * mesh_rows
        and mesh_rows > 2
        and power_of_two(mesh_rows)
        and block_columns.shape[0] >= 2 * REACH + 2
    )
    step = paired_step if fits else general_step
    return step(covariance, couplings, block_columns, onsite)


def solution(mesh):
    return jax.shard_map(
        on_device,
        mesh=mesh,
        in_specs=(P("row", "col"), P("row", None, None, None), P(), P()),
        out_specs=P("row", "col"),
        check_vma=False,
    )
```

```python
import functools

import jax
import jax.numpy as jnp
from jax import lax
from jax.experimental import pallas as pl
from jax.experimental.pallas import tpu as pltpu
from jax.sharding import PartitionSpec as P

BLOCK = 128
REACH = 5


step_size = 0.25


def from_root(block, axis, holder):
    block = jnp.where(lax.axis_index(axis) == holder, block, jnp.zeros_like(block))
    return lax.psum(block, axis)


def shifted(block, axis, distance):
    devices = range(lax.axis_size(axis))
    route = [((i - distance) % len(devices), i) for i in devices]
    return lax.ppermute(block, axis, route)


def relative_positions(columns, first_block, count, total_blocks):
    own_ids = first_block + jnp.arange(count, dtype=jnp.int32)
    relative = (columns - own_ids[:, None] + total_blocks // 2) % total_blocks - total_blocks // 2
    return jnp.arange(count, dtype=jnp.int32)[:, None] + relative + REACH


def general_step(covariance, couplings, block_columns, onsite):
    tile_rows, tile_cols = covariance.shape
    row_blocks = tile_rows // BLOCK
    col_blocks = tile_cols // BLOCK
    total_blocks = block_columns.shape[0]
    reach_cells = REACH * BLOCK
    row_hops = -(-reach_cells // tile_rows)
    col_hops = -(-reach_cells // tile_cols)
    first_row = lax.axis_index("row") * row_blocks
    first_col = lax.axis_index("col") * col_blocks
    own_offset = jnp.clip(first_col - first_row, 0, row_blocks - col_blocks)
    col_root = first_col // row_blocks
    own_couplings = lax.dynamic_slice_in_dim(couplings, own_offset, col_blocks, 0)
    col_couplings = from_root(own_couplings, "row", col_root)
    row_columns = lax.dynamic_slice_in_dim(block_columns, first_row, row_blocks, 0)
    col_columns = lax.dynamic_slice_in_dim(block_columns, first_col, col_blocks, 0)
    row_positions = relative_positions(row_columns, first_row, row_blocks, total_blocks)
    col_positions = relative_positions(col_columns, first_col, col_blocks, total_blocks)
    row_gains = lax.dynamic_slice_in_dim(onsite, first_row, row_blocks, 0)
    col_gains = lax.dynamic_slice_in_dim(onsite, first_col, col_blocks, 0)
    middle = covariance
    shaped = middle.reshape(row_blocks, BLOCK, col_blocks, BLOCK)
    picked = lax.dynamic_slice_in_dim(shaped, own_offset, col_blocks, 0)
    indices = jnp.arange(col_blocks, dtype=jnp.int32)
    local_diagonal = picked[indices, :, indices, :]
    received = []
    for root_part in range(row_blocks // col_blocks):
        received.append(from_root(local_diagonal, "col", first_row // col_blocks + root_part))
    row_diagonal = jnp.concatenate(received, axis=0)
    lower_parts = []
    upper_parts = []
    for distance in range(1, row_hops + 1):
        needed = min(tile_rows, reach_cells - (distance - 1) * tile_rows)
        to_upper = middle[tile_rows - needed :]
        to_lower = middle[:needed]
        from_lower = shifted(to_upper, "row", distance)
        from_upper = shifted(to_lower, "row", -distance)
        lower_parts.insert(0, from_lower)
        upper_parts.append(from_upper)
    extended_rows = jnp.concatenate(lower_parts + [middle] + upper_parts, axis=0).reshape(
        -1, BLOCK, tile_cols
    )
    picked_rows = jnp.take(extended_rows, row_positions, axis=0)
    left_part = jnp.einsum(
        "ikab,ikbn->ian", couplings, picked_rows, precision=lax.Precision.HIGHEST
    )
    left_part = left_part + jnp.einsum(
        "iab,ibn->ian",
        row_diagonal * row_gains[:, None, None],
        middle.reshape(row_blocks, BLOCK, tile_cols),
        precision=lax.Precision.HIGHEST,
    )
    left_part = left_part.reshape(tile_rows, tile_cols)
    col_diagonal = from_root(local_diagonal, "row", col_root)
    left_parts = []
    right_parts = []
    for distance in range(1, col_hops + 1):
        needed = min(tile_cols, reach_cells - (distance - 1) * tile_cols)
        to_right = middle[:, tile_cols - needed :]
        to_left = middle[:, :needed]
        from_left = shifted(to_right, "col", distance)
        from_right = shifted(to_left, "col", -distance)
        left_parts.insert(0, from_left)
        right_parts.append(from_right)
    extended_cols = jnp.concatenate(left_parts + [middle] + right_parts, axis=1).reshape(
        tile_rows, -1, BLOCK
    )
    picked_cols = jnp.take(extended_cols, col_positions, axis=1)
    right_part = jnp.einsum(
        "nikb,ikab->nia", picked_cols, col_couplings, precision=lax.Precision.HIGHEST
    )
    right_part = right_part + jnp.einsum(
        "nib,iab->nia",
        middle.reshape(tile_rows, col_blocks, BLOCK),
        col_diagonal * col_gains[:, None, None],
        precision=lax.Precision.HIGHEST,
    )
    right_part = right_part.reshape(tile_rows, tile_cols)
    return covariance + step_size * (left_part + right_part)


GROUP = 2
WINDOW = (GROUP + 2 * REACH) * BLOCK
HALO = REACH * BLOCK
VMEM = 56 * 1024 * 1024
SHORT = pl.CostEstimate(flops=1, bytes_accessed=1, transcendentals=0)
LONG = pl.CostEstimate(flops=4 * 10**11, bytes_accessed=16 * 10**8, transcendentals=0)


def halves(value):
    high = value.astype(jnp.bfloat16)
    return high, (value - high.astype(jnp.float32)).astype(jnp.bfloat16)


def product(a_high, a_low, b_high, b_low, contract_b=0):
    dims = (((1,), (contract_b,)), ((), ()))
    dot = functools.partial(lax.dot_general, dimension_numbers=dims, preferred_element_type=jnp.float32)
    return dot(a_high, b_high) + (dot(a_high, b_low) + dot(a_low, b_high))


def band_kernel(places, gains, scalars, *refs, sources, half):
    blocks, diagonals, (high, low, whole) = refs[:sources], refs[sources:-3], refs[-3:]
    i = pl.program_id(0)
    whole[...] = jnp.zeros_like(whole)
    down = lax.broadcasted_iota(jnp.int32, (BLOCK, BLOCK), 0)
    across = lax.broadcasted_iota(jnp.int32, (BLOCK, BLOCK), 1)
    beyond = jnp.where(i % (2 * half) < half, across - down, down - across)
    own = pl.multiple_of((REACH + i % GROUP) * BLOCK, BLOCK)
    for source in range(sources):

        @pl.when(scalars[0] == source)
        def _():
            for k in range(blocks[source].shape[0]):
                place = pl.multiple_of(places[i, k] * BLOCK, BLOCK)
                whole[:, pl.ds(place, BLOCK)] = blocks[source][k]
            if diagonals:
                part = jnp.where(beyond > 0, diagonals[source][0], 0.0)
                whole[:, pl.ds(own, BLOCK)] += gains[i] * (part - part.T)

    high[...], low[...] = halves(whole[...])


def band(sources, choice, offset, diagonals, diagonal_offset, half, columns, first_block, total_blocks, gains):
    count, stored = columns.shape
    own_ids = first_block + jnp.arange(count, dtype=jnp.int32)
    relative = (columns - own_ids[:, None] + total_blocks // 2) % total_blocks - total_blocks // 2
    places = relative + REACH + (jnp.arange(count, dtype=jnp.int32) % GROUP)[:, None]
    shape = jax.ShapeDtypeStruct((count * BLOCK, WINDOW), jnp.bfloat16)

    def blocks_of(source):
        def index(i, places, gains, scalars):
            return (jnp.where(scalars[0] == source, scalars[1] + i, 0), 0, 0)

        return pl.BlockSpec((stored, BLOCK, BLOCK), index)

    def diagonal_of(source):
        def index(i, places, gains, scalars):
            return (jnp.where(scalars[0] == source, scalars[2] + i // (2 * half) * half + i % half, 0), 0, 0)

        return pl.BlockSpec((1, BLOCK, BLOCK), index)

    return pl.pallas_call(
        functools.partial(band_kernel, sources=len(sources), half=half),
        out_shape=(shape, shape),
        grid_spec=pltpu.PrefetchScalarGridSpec(
            num_scalar_prefetch=3,
            grid=(count,),
            in_specs=[blocks_of(j) for j in range(len(sources))] + [diagonal_of(j) for j in range(len(diagonals))],
            out_specs=[pl.BlockSpec((BLOCK, WINDOW), lambda i, *_: (i, 0))] * 2,
            scratch_shapes=[pltpu.VMEM((BLOCK, WINDOW), jnp.float32)],
        ),
        compiler_params=pltpu.CompilerParams(vmem_limit_bytes=VMEM),
        cost_estimate=SHORT,
        name="band",
    )(places, gains, jnp.stack([choice, offset, diagonal_offset]).astype(jnp.int32), *sources, *diagonals)


def onsite_kernel(gains, *refs, half):
    diagonals, (high, low, new_high, new_low) = refs[:GROUP], refs[GROUP:]
    g = pl.program_id(0)
    down = lax.broadcasted_iota(jnp.int32, (BLOCK, BLOCK), 0)
    across = lax.broadcasted_iota(jnp.int32, (BLOCK, BLOCK), 1)
    new_high[...], new_low[...] = high[...], low[...]
    for b, diagonal in enumerate(diagonals):
        i = g * GROUP + b
        here = slice(b * BLOCK, (b + 1) * BLOCK)
        beyond = jnp.where(i % (2 * half) < half, across - down, down - across)
        part = jnp.where(beyond > 0, diagonal[0], 0.0)
        value = high[here, here].astype(jnp.float32) + low[here, here].astype(jnp.float32)
        new_high[here, here], new_low[here, here] = halves(value + gains[i] * (part - part.T))


def add_onsite(high, low, diagonals, half, gains):
    step = GROUP * BLOCK
    own = pl.BlockSpec((pl.Element(step), pl.Element(step)), lambda g, gains: (g * step, HALO))
    shape = jax.ShapeDtypeStruct(high.shape, high.dtype)

    def diagonal_of(b):
        def index(g, gains):
            i = g * GROUP + b
            return (i // (2 * half) * half + i % half, 0, 0)

        return pl.BlockSpec((1, BLOCK, BLOCK), index)

    return pl.pallas_call(
        functools.partial(onsite_kernel, half=half),
        out_shape=(shape, shape),
        grid_spec=pltpu.PrefetchScalarGridSpec(
            num_scalar_prefetch=1,
            grid=(high.shape[0] // step,),
            in_specs=[diagonal_of(b) for b in range(GROUP)] + [own, own],
            out_specs=[own, own],
        ),
        input_output_aliases={1 + GROUP: 0, 2 + GROUP: 1},
        compiler_params=pltpu.CompilerParams(vmem_limit_bytes=VMEM),
        cost_estimate=SHORT,
        name="add_onsite",
    )(gains, *([diagonals] * GROUP), high, low)


def left_kernel(up, inner, own, outer, high, low, out, ext_high, ext_low):
    rows = own.shape[0]
    top = jnp.where(up[0] == 0, outer[...], inner[...])
    bottom = jnp.where(up[0] == 0, inner[...], outer[...])
    for start, part in ((0, top), (HALO, own[...]), (HALO + rows, bottom)):
        size = part.shape[0]
        ext_high[start : start + size], ext_low[start : start + size] = halves(part)
    step = GROUP * BLOCK
    for g in range(rows // step):
        here, window = slice(g * step, (g + 1) * step), slice(g * step, g * step + WINDOW)
        value = product(high[here], low[here], ext_high[window], ext_low[window])
        out[here] = own[here] + step_size * value


def left_part(up, inner, covariance, outer, high, low, slab=2 * BLOCK):
    rows, cols = covariance.shape
    whole = pl.BlockSpec((rows, WINDOW), lambda j, s: (0, 0), pipeline_mode=pl.Buffered(1))
    beyond = pl.BlockSpec((HALO, slab), lambda j, s: (0, j))
    here = pl.BlockSpec((rows, slab), lambda j, s: (0, j))
    return pl.pallas_call(
        left_kernel,
        out_shape=jax.ShapeDtypeStruct((rows, cols), jnp.float32),
        grid_spec=pltpu.PrefetchScalarGridSpec(
            num_scalar_prefetch=1,
            grid=(cols // slab,),
            in_specs=[beyond, here, beyond, whole, whole],
            out_specs=here,
            scratch_shapes=[pltpu.VMEM((rows + 2 * HALO, slab), jnp.bfloat16)] * 2,
        ),
        compiler_params=pltpu.CompilerParams(vmem_limit_bytes=VMEM),
        cost_estimate=SHORT,
        name="left_part",
    )(up.reshape(1).astype(jnp.int32), inner, covariance, outer, high, low)


def right_kernel(odd, pair, strip, own, high, low, total, out, ext_high, ext_low):
    rows, cols = own.shape

    def put(start, value):
        end = start + value.shape[1]
        ext_high[:, start:end], ext_low[:, start:end] = halves(value)

    put(HALO, own[...])

    @pl.when(odd[0] == 0)
    def _():
        put(0, strip[...])
        put(HALO + cols, pair[:, :HALO])

    @pl.when(odd[0] == 1)
    def _():
        put(0, pair[:, cols - HALO :])
        put(HALO + cols, strip[...])

    step = GROUP * BLOCK
    for g in range(cols // step):
        here, window = slice(g * step, (g + 1) * step), slice(g * step, g * step + WINDOW)
        value = product(ext_high[:, window], ext_low[:, window], high[here], low[here], 1)
        out[:, here] = total[:, here] + step_size * value


def right_part(first, odd, pair, strip, covariance, high, low, total, rows):
    cols = covariance.shape[1]
    count = pair.shape[0] // rows
    scalars = jnp.stack([odd, first]).astype(jnp.int32)
    whole = pl.BlockSpec(high.shape, lambda j, s: (0, 0), pipeline_mode=pl.Buffered(1))
    there = pl.BlockSpec((pl.Element(rows), pl.Element(cols)), lambda j, s: (pl.multiple_of(s[1] + j * rows, BLOCK), 0))
    return pl.pallas_call(
        right_kernel,
        out_shape=jax.ShapeDtypeStruct(total.shape, jnp.float32),
        grid_spec=pltpu.PrefetchScalarGridSpec(
            num_scalar_prefetch=1,
            grid=(count,),
            in_specs=[
                pl.BlockSpec((rows, cols), lambda j, s: (j, 0)),
                pl.BlockSpec((rows, HALO), lambda j, s: (j, 0)),
                there,
                whole,
                whole,
                there,
            ],
            out_specs=there,
            scratch_shapes=[pltpu.VMEM((rows, cols + 2 * HALO), jnp.bfloat16)] * 2,
        ),
        input_output_aliases={6: 0},
        compiler_params=pltpu.CompilerParams(vmem_limit_bytes=VMEM),
        cost_estimate=SHORT,
        name="right_part",
    )(scalars, pair, strip, covariance, high, low, total)


def send(value, pairs, cols):
    return lax.ppermute(value, ("row", "col"), [(a * cols + b, c * cols + d) for (a, b), (c, d) in pairs])


def cols_route(hop, devices, ratio):
    return [
        ((r, c), (r, ((c // ratio) ^ hop) * ratio + c % ratio))
        for r, c in devices
        if ((c // ratio) ^ r) & (2 * hop - 1) == 0
    ]


def cut(total):
    first = total * 5 // 16 // BLOCK * BLOCK
    sizes = [first, first]
    left = total - 2 * first
    while left > BLOCK:
        sizes.append(-(-left // (2 * BLOCK)) * BLOCK)
        left -= sizes[-1]
    return sizes + [left] * (left > 0)


def rows_kernel(first, rows, out):
    out[...] = rows[...]


def rows_of(covariance, first, size):
    cols = covariance.shape[1]
    step = size // 2 if size % (16 * BLOCK // 8) == 0 else size
    return pl.pallas_call(
        rows_kernel,
        out_shape=jax.ShapeDtypeStruct((size, cols), covariance.dtype),
        grid_spec=pltpu.PrefetchScalarGridSpec(
            num_scalar_prefetch=1,
            grid=(size // step,),
            in_specs=[pl.BlockSpec((pl.Element(step), pl.Element(cols)), lambda j, s: (pl.multiple_of(s[0] + j * step, 8), 0))],
            out_specs=pl.BlockSpec((step, cols), lambda j, s: (j, 0)),
        ),
        cost_estimate=SHORT,
        name="rows_of",
    )(jnp.asarray(first, jnp.int32).reshape(1), covariance)


def packed_kernel(first, upper, lower, out):
    across = lax.broadcasted_iota(jnp.int32, (BLOCK, BLOCK), 1)
    down = lax.broadcasted_iota(jnp.int32, (BLOCK, BLOCK), 0)
    out[0] = jnp.where(across > down, upper[...], jnp.where(across < down, lower[...], 0.0))


def packed_diagonal(covariance, first, count):
    half = count // 2
    return pl.pallas_call(
        packed_kernel,
        out_shape=jax.ShapeDtypeStruct((half, BLOCK, BLOCK), jnp.float32),
        grid_spec=pltpu.PrefetchScalarGridSpec(
            num_scalar_prefetch=1,
            grid=(half,),
            in_specs=[
                pl.BlockSpec((BLOCK, BLOCK), lambda j, s: (s[0] + j, j)),
                pl.BlockSpec((BLOCK, BLOCK), lambda j, s: (s[0] + half + j, half + j)),
            ],
            out_specs=pl.BlockSpec((1, BLOCK, BLOCK), lambda j, s: (j, 0, 0)),
        ),
        cost_estimate=SHORT,
        name="packed_diagonal",
    )(first.reshape(1).astype(jnp.int32), covariance, covariance)


def gate_kernel(*refs):
    pass


def gate(*arrays, cost=SHORT):
    shapes = tuple(jax.ShapeDtypeStruct(array.shape, array.dtype) for array in arrays)
    anywhere = [pl.BlockSpec(memory_space=pl.ANY)] * len(arrays)
    return pl.pallas_call(
        gate_kernel,
        out_shape=shapes,
        in_specs=anywhere,
        out_specs=tuple(anywhere),
        input_output_aliases={j: j for j in range(len(arrays))},
        cost_estimate=cost,
        name="gate",
    )(*arrays)


def paired_step(covariance, couplings, block_columns, onsite):
    tile_rows, tile_cols = covariance.shape
    row_blocks, col_blocks = tile_rows // BLOCK, tile_cols // BLOCK
    total_blocks, stored = block_columns.shape
    mesh_rows, mesh_cols = lax.axis_size("row"), lax.axis_size("col")
    ratio = tile_rows // tile_cols
    row, col = lax.axis_index("row"), lax.axis_index("col")
    odd, up = col % 2, row % 2
    first_row, first_col = row * row_blocks, col * col_blocks
    offset = jnp.clip(first_col - first_row, 0, row_blocks - col_blocks)
    devices = [(r, c) for r in range(mesh_rows) for c in range(mesh_cols)]
    partners = [((r, c), (r, c ^ 1)) for r, c in devices]
    next_pairs = [((r, c), (r, (c + (2 if c % 2 == 0 else -2)) % mesh_cols)) for r, c in devices]
    inner_route = [((r, c), (r ^ 1, c)) for r, c in devices]
    outer_route = [((r, c), ((r + (-1 if r % 2 == 0 else 1)) % mesh_rows, c)) for r, c in devices]
    beside = 0
    sizes = cut(tile_rows - beside)
    firsts = [sum(sizes[:j]) for j in range(len(sizes))]
    chunks = {j: rows_of(covariance, firsts[j], sizes[j]) for j in range(len(sizes))}
    pairs, strips = {}, {}

    def move(value, route):
        return send(value, route, mesh_cols)

    def exchange(*numbers):
        for j in numbers:
            if j < len(sizes):
                pairs[j] = move(chunks[j], partners)

    def hand_strip_on(j):
        strip = lax.dynamic_slice_in_dim(pairs[j], (1 - odd) * (tile_cols - HALO), HALO, 1)
        strips[j] = move(strip, next_pairs)

    def add_right(total, j):
        first = jnp.int32(firsts[j])
        return right_part(first, odd, pairs[j], strips[j], covariance, col_high, col_low, total, sizes[j])

    diagonal = packed_diagonal(covariance, offset, col_blocks)
    other = move(diagonal, [((r, c), (r, c ^ 1)) for r, c in devices if c // 2 == r])
    far = tile_rows - HALO
    outer = move(rows_of(covariance, up * far, HALO), outer_route)
    other, chunks[0] = gate(other, chunks[0])
    exchange(0)
    inner = move(rows_of(covariance, (1 - up) * far, HALO), inner_route)
    both = jnp.where(odd == 0, jnp.stack([diagonal, other]), jnp.stack([other, diagonal]))
    both = both.reshape(-1, BLOCK, BLOCK)
    across, hop = (col // ratio) ^ row, mesh_cols // ratio // 2
    while hop:
        (moved,) = gate(move(both, cols_route(hop, devices, ratio)))
        both = jnp.where(across & (2 * hop - 1) == hop, moved, both)
        hop //= 2
    zero = jnp.int32(0)
    half = col_blocks // 2
    blocks = couplings.reshape(-1, BLOCK, BLOCK)
    columns = lax.dynamic_slice_in_dim(block_columns, first_row, row_blocks, 0)
    row_gains = lax.dynamic_slice_in_dim(onsite, first_row, row_blocks, 0)
    row_high, row_low = band([blocks], zero, zero, [], zero, half, columns, first_row, total_blocks, row_gains)
    row_high, row_low = add_onsite(row_high, row_low, both, half, row_gains)
    count = col_blocks * stored
    own_blocks = lax.dynamic_slice_in_dim(blocks, offset * stored, count, 0)
    held = {0: jnp.concatenate([own_blocks, diagonal], axis=0)}

    def hand_on(place):
        low = place & -place
        route = [((r, c), (r ^ low, c)) for r, c in devices if r ^ (c // ratio) == place ^ low]
        held[place] = move(held[place ^ low], route)

    places = sorted(range(1, mesh_rows), key=lambda place: (bin(place).count("1"), -place))
    nearest = [place for place in places if place & (place - 1) == 0]

    pairs[0], outer = gate(pairs[0], outer, cost=LONG)
    pairs[0], chunks[1], outer, inner, row_high, held[0] = gate(
        pairs[0], chunks[1], outer, inner, row_high, held[0]
    )
    exchange(1)
    for place in nearest:
        hand_on(place)
    hand_strip_on(0)
    total = left_part(up, inner, covariance, outer, row_high, row_low)

    (pairs[1],) = gate(pairs[1], cost=LONG)
    pairs[1], strips[0], total, chunks[2], chunks[3], *got = gate(
        pairs[1], strips[0], total, chunks[2], chunks[3], *(held[place] for place in nearest)
    )
    held.update(zip(nearest, got))
    for place in places[len(nearest) :]:
        hand_on(place)
    exchange(2, 3)
    hand_strip_on(1)
    sources = [held[place] for place in range(mesh_rows)]
    columns = lax.dynamic_slice_in_dim(block_columns, first_col, col_blocks, 0)
    gains = lax.dynamic_slice_in_dim(onsite, first_col, col_blocks, 0)
    col_high, col_low = band(
        sources, row ^ (col // ratio), zero, sources, jnp.int32(count), half, columns, first_col, total_blocks, gains
    )
    total = add_right(total, 0)
    for j in range(2, len(sizes)):
        if j + 2 < len(sizes):
            pairs[j], total, chunks[j + 2] = gate(pairs[j], total, chunks[j + 2])
        else:
            pairs[j], total = gate(pairs[j], total)
        hand_strip_on(j)
        exchange(j + 2)
        total = add_right(total, j - 1)
    return add_right(total, len(sizes) - 1)


def power_of_two(number):
    return number & (number - 1) == 0


def on_device(covariance, couplings, block_columns, onsite):
    tile_rows, tile_cols = covariance.shape
    mesh_rows, mesh_cols = lax.axis_size("row"), lax.axis_size("col")
    fits = (
        tile_cols >= HALO
        and tile_cols % (GROUP * BLOCK) == 0
        and tile_rows == 2 * tile_cols
        and mesh_cols == 2 * mesh_rows
        and mesh_rows > 2
        and power_of_two(mesh_rows)
        and block_columns.shape[0] >= 2 * REACH + 2
    )
    step = paired_step if fits else general_step
    return step(covariance, couplings, block_columns, onsite)


def solution(mesh):
    return jax.shard_map(
        on_device,
        mesh=mesh,
        in_specs=(P("row", "col"), P("row", None, None, None), P(), P()),
        out_specs=P("row", "col"),
        check_vma=False,
    )
```

```python
import functools

import jax
import jax.numpy as jnp
from jax import lax
from jax.experimental import pallas as pl
from jax.experimental.pallas import tpu as pltpu
from jax.sharding import PartitionSpec as P

BLOCK = 128
REACH = 5


step_size = 0.25


def from_root(block, axis, holder):
    block = jnp.where(lax.axis_index(axis) == holder, block, jnp.zeros_like(block))
    return lax.psum(block, axis)


def shifted(block, axis, distance):
    devices = range(lax.axis_size(axis))
    route = [((i - distance) % len(devices), i) for i in devices]
    return lax.ppermute(block, axis, route)


def relative_positions(columns, first_block, count, total_blocks):
    own_ids = first_block + jnp.arange(count, dtype=jnp.int32)
    relative = (columns - own_ids[:, None] + total_blocks // 2) % total_blocks - total_blocks // 2
    return jnp.arange(count, dtype=jnp.int32)[:, None] + relative + REACH


def general_step(covariance, couplings, block_columns, onsite):
    tile_rows, tile_cols = covariance.shape
    row_blocks = tile_rows // BLOCK
    col_blocks = tile_cols // BLOCK
    total_blocks = block_columns.shape[0]
    reach_cells = REACH * BLOCK
    row_hops = -(-reach_cells // tile_rows)
    col_hops = -(-reach_cells // tile_cols)
    first_row = lax.axis_index("row") * row_blocks
    first_col = lax.axis_index("col") * col_blocks
    own_offset = jnp.clip(first_col - first_row, 0, row_blocks - col_blocks)
    col_root = first_col // row_blocks
    own_couplings = lax.dynamic_slice_in_dim(couplings, own_offset, col_blocks, 0)
    col_couplings = from_root(own_couplings, "row", col_root)
    row_columns = lax.dynamic_slice_in_dim(block_columns, first_row, row_blocks, 0)
    col_columns = lax.dynamic_slice_in_dim(block_columns, first_col, col_blocks, 0)
    row_positions = relative_positions(row_columns, first_row, row_blocks, total_blocks)
    col_positions = relative_positions(col_columns, first_col, col_blocks, total_blocks)
    row_gains = lax.dynamic_slice_in_dim(onsite, first_row, row_blocks, 0)
    col_gains = lax.dynamic_slice_in_dim(onsite, first_col, col_blocks, 0)
    middle = covariance
    shaped = middle.reshape(row_blocks, BLOCK, col_blocks, BLOCK)
    picked = lax.dynamic_slice_in_dim(shaped, own_offset, col_blocks, 0)
    indices = jnp.arange(col_blocks, dtype=jnp.int32)
    local_diagonal = picked[indices, :, indices, :]
    received = []
    for root_part in range(row_blocks // col_blocks):
        received.append(from_root(local_diagonal, "col", first_row // col_blocks + root_part))
    row_diagonal = jnp.concatenate(received, axis=0)
    lower_parts = []
    upper_parts = []
    for distance in range(1, row_hops + 1):
        needed = min(tile_rows, reach_cells - (distance - 1) * tile_rows)
        to_upper = middle[tile_rows - needed :]
        to_lower = middle[:needed]
        from_lower = shifted(to_upper, "row", distance)
        from_upper = shifted(to_lower, "row", -distance)
        lower_parts.insert(0, from_lower)
        upper_parts.append(from_upper)
    extended_rows = jnp.concatenate(lower_parts + [middle] + upper_parts, axis=0).reshape(
        -1, BLOCK, tile_cols
    )
    picked_rows = jnp.take(extended_rows, row_positions, axis=0)
    left_part = jnp.einsum(
        "ikab,ikbn->ian", couplings, picked_rows, precision=lax.Precision.HIGHEST
    )
    left_part = left_part + jnp.einsum(
        "iab,ibn->ian",
        row_diagonal * row_gains[:, None, None],
        middle.reshape(row_blocks, BLOCK, tile_cols),
        precision=lax.Precision.HIGHEST,
    )
    left_part = left_part.reshape(tile_rows, tile_cols)
    col_diagonal = from_root(local_diagonal, "row", col_root)
    left_parts = []
    right_parts = []
    for distance in range(1, col_hops + 1):
        needed = min(tile_cols, reach_cells - (distance - 1) * tile_cols)
        to_right = middle[:, tile_cols - needed :]
        to_left = middle[:, :needed]
        from_left = shifted(to_right, "col", distance)
        from_right = shifted(to_left, "col", -distance)
        left_parts.insert(0, from_left)
        right_parts.append(from_right)
    extended_cols = jnp.concatenate(left_parts + [middle] + right_parts, axis=1).reshape(
        tile_rows, -1, BLOCK
    )
    picked_cols = jnp.take(extended_cols, col_positions, axis=1)
    right_part = jnp.einsum(
        "nikb,ikab->nia", picked_cols, col_couplings, precision=lax.Precision.HIGHEST
    )
    right_part = right_part + jnp.einsum(
        "nib,iab->nia",
        middle.reshape(tile_rows, col_blocks, BLOCK),
        col_diagonal * col_gains[:, None, None],
        precision=lax.Precision.HIGHEST,
    )
    right_part = right_part.reshape(tile_rows, tile_cols)
    return covariance + step_size * (left_part + right_part)


GROUP = 2
WINDOW = (GROUP + 2 * REACH) * BLOCK
HALO = REACH * BLOCK
VMEM = 56 * 1024 * 1024
SHORT = pl.CostEstimate(flops=1, bytes_accessed=1, transcendentals=0)
SOME = pl.CostEstimate(flops=10**10, bytes_accessed=4 * 10**7, transcendentals=0)
LONG = pl.CostEstimate(flops=4 * 10**11, bytes_accessed=16 * 10**8, transcendentals=0)


def halves(value):
    high = value.astype(jnp.bfloat16)
    return high, (value - high.astype(jnp.float32)).astype(jnp.bfloat16)


def product(a_high, a_low, b_high, b_low, contract_b=0):
    dims = (((1,), (contract_b,)), ((), ()))
    dot = functools.partial(lax.dot_general, dimension_numbers=dims, preferred_element_type=jnp.float32)
    return dot(a_high, b_high) + (dot(a_high, b_low) + dot(a_low, b_high))


def band_kernel(places, gains, scalars, *refs, sources, half):
    blocks, diagonals, (high, low, whole) = refs[:sources], refs[sources:-3], refs[-3:]
    i = pl.program_id(0)
    whole[...] = jnp.zeros_like(whole)
    down = lax.broadcasted_iota(jnp.int32, (BLOCK, BLOCK), 0)
    across = lax.broadcasted_iota(jnp.int32, (BLOCK, BLOCK), 1)
    beyond = jnp.where(i % (2 * half) < half, across - down, down - across)
    own = pl.multiple_of((REACH + i % GROUP) * BLOCK, BLOCK)
    for source in range(sources):

        @pl.when(scalars[0] == source)
        def _():
            for k in range(blocks[source].shape[0]):
                place = pl.multiple_of(places[i, k] * BLOCK, BLOCK)
                whole[:, pl.ds(place, BLOCK)] = blocks[source][k]
            if diagonals:
                part = jnp.where(beyond > 0, diagonals[source][0], 0.0)
                whole[:, pl.ds(own, BLOCK)] += gains[i] * (part - part.T)

    high[...], low[...] = halves(whole[...])


def band(sources, choice, offset, diagonals, diagonal_offset, half, columns, first_block, total_blocks, gains):
    count, stored = columns.shape
    own_ids = first_block + jnp.arange(count, dtype=jnp.int32)
    relative = (columns - own_ids[:, None] + total_blocks // 2) % total_blocks - total_blocks // 2
    places = relative + REACH + (jnp.arange(count, dtype=jnp.int32) % GROUP)[:, None]
    shape = jax.ShapeDtypeStruct((count * BLOCK, WINDOW), jnp.bfloat16)

    def blocks_of(source):
        def index(i, places, gains, scalars):
            return (jnp.where(scalars[0] == source, scalars[1] + i, 0), 0, 0)

        return pl.BlockSpec((stored, BLOCK, BLOCK), index)

    def diagonal_of(source):
        def index(i, places, gains, scalars):
            return (jnp.where(scalars[0] == source, scalars[2] + i // (2 * half) * half + i % half, 0), 0, 0)

        return pl.BlockSpec((1, BLOCK, BLOCK), index)

    return pl.pallas_call(
        functools.partial(band_kernel, sources=len(sources), half=half),
        out_shape=(shape, shape),
        grid_spec=pltpu.PrefetchScalarGridSpec(
            num_scalar_prefetch=3,
            grid=(count,),
            in_specs=[blocks_of(j) for j in range(len(sources))] + [diagonal_of(j) for j in range(len(diagonals))],
            out_specs=[pl.BlockSpec((BLOCK, WINDOW), lambda i, *_: (i, 0))] * 2,
            scratch_shapes=[pltpu.VMEM((BLOCK, WINDOW), jnp.float32)],
        ),
        compiler_params=pltpu.CompilerParams(vmem_limit_bytes=VMEM),
        cost_estimate=SHORT,
        name="band",
    )(places, gains, jnp.stack([choice, offset, diagonal_offset]).astype(jnp.int32), *sources, *diagonals)


def onsite_kernel(gains, *refs, half):
    diagonals, (high, low, new_high, new_low) = refs[:GROUP], refs[GROUP:]
    g = pl.program_id(0)
    down = lax.broadcasted_iota(jnp.int32, (BLOCK, BLOCK), 0)
    across = lax.broadcasted_iota(jnp.int32, (BLOCK, BLOCK), 1)
    new_high[...], new_low[...] = high[...], low[...]
    for b, diagonal in enumerate(diagonals):
        i = g * GROUP + b
        here = slice(b * BLOCK, (b + 1) * BLOCK)
        beyond = jnp.where(i % (2 * half) < half, across - down, down - across)
        part = jnp.where(beyond > 0, diagonal[0], 0.0)
        value = high[here, here].astype(jnp.float32) + low[here, here].astype(jnp.float32)
        new_high[here, here], new_low[here, here] = halves(value + gains[i] * (part - part.T))


def add_onsite(high, low, diagonals, half, gains):
    step = GROUP * BLOCK
    own = pl.BlockSpec((pl.Element(step), pl.Element(step)), lambda g, gains: (g * step, HALO))
    shape = jax.ShapeDtypeStruct(high.shape, high.dtype)

    def diagonal_of(b):
        def index(g, gains):
            i = g * GROUP + b
            return (i // (2 * half) * half + i % half, 0, 0)

        return pl.BlockSpec((1, BLOCK, BLOCK), index)

    return pl.pallas_call(
        functools.partial(onsite_kernel, half=half),
        out_shape=(shape, shape),
        grid_spec=pltpu.PrefetchScalarGridSpec(
            num_scalar_prefetch=1,
            grid=(high.shape[0] // step,),
            in_specs=[diagonal_of(b) for b in range(GROUP)] + [own, own],
            out_specs=[own, own],
        ),
        input_output_aliases={1 + GROUP: 0, 2 + GROUP: 1},
        compiler_params=pltpu.CompilerParams(vmem_limit_bytes=VMEM),
        cost_estimate=SHORT,
        name="add_onsite",
    )(gains, *([diagonals] * GROUP), high, low)


def left_kernel(up, inner, own, outer, high, low, out, ext_high, ext_low):
    rows = own.shape[0]
    top = jnp.where(up[0] == 0, outer[...], inner[...])
    bottom = jnp.where(up[0] == 0, inner[...], outer[...])
    for start, part in ((0, top), (HALO, own[...]), (HALO + rows, bottom)):
        size = part.shape[0]
        ext_high[start : start + size], ext_low[start : start + size] = halves(part)
    step = GROUP * BLOCK
    for g in range(rows // step):
        here, window = slice(g * step, (g + 1) * step), slice(g * step, g * step + WINDOW)
        value = product(high[here], low[here], ext_high[window], ext_low[window])
        out[here] = own[here] + step_size * value


def left_part(up, inner, covariance, outer, high, low, slab=2 * BLOCK):
    rows, cols = covariance.shape
    whole = pl.BlockSpec((rows, WINDOW), lambda j, s: (0, 0), pipeline_mode=pl.Buffered(1))
    beyond = pl.BlockSpec((HALO, slab), lambda j, s: (0, j))
    here = pl.BlockSpec((rows, slab), lambda j, s: (0, j))
    return pl.pallas_call(
        left_kernel,
        out_shape=jax.ShapeDtypeStruct((rows, cols), jnp.float32),
        grid_spec=pltpu.PrefetchScalarGridSpec(
            num_scalar_prefetch=1,
            grid=(cols // slab,),
            in_specs=[beyond, here, beyond, whole, whole],
            out_specs=here,
            scratch_shapes=[pltpu.VMEM((rows + 2 * HALO, slab), jnp.bfloat16)] * 2,
        ),
        compiler_params=pltpu.CompilerParams(vmem_limit_bytes=VMEM),
        cost_estimate=SHORT,
        name="left_part",
    )(up.reshape(1).astype(jnp.int32), inner, covariance, outer, high, low)


def right_kernel(scalars, pair, strip, own, high, low, total, out, ext_high, ext_low):
    cols = own.shape[1]

    def put(start, value):
        end = start + value.shape[1]
        ext_high[:, start:end], ext_low[:, start:end] = halves(value)

    g = pl.program_id(0)

    @pl.when(g == 0)
    def _():
        put(HALO, own[...])

    @pl.when((g == 0) & (scalars[0] == 0))
    def _():
        put(0, strip[...])
        put(HALO + cols, pair[:, :HALO])

    @pl.when((g == 0) & (scalars[0] == 1))
    def _():
        put(0, pair[:, cols - HALO :])
        put(HALO + cols, strip[...])

    window = pl.ds(pl.multiple_of(g * (GROUP * BLOCK), GROUP * BLOCK), WINDOW)
    value = product(ext_high[:, window], ext_low[:, window], high[...], low[...], 1)
    out[...] = total[...] + step_size * value


def right_part(first, odd, pair, strip, covariance, high, low, total):
    rows, cols = pair.shape
    step = GROUP * BLOCK
    scalars = jnp.stack([odd, first]).astype(jnp.int32)
    band_rows = pl.BlockSpec((step, WINDOW), lambda g, s: (g, 0))
    here = pl.BlockSpec((pl.Element(rows), pl.Element(step)), lambda g, s: (pl.multiple_of(s[1], BLOCK), g * step))
    return pl.pallas_call(
        right_kernel,
        out_shape=jax.ShapeDtypeStruct(total.shape, jnp.float32),
        grid_spec=pltpu.PrefetchScalarGridSpec(
            num_scalar_prefetch=1,
            grid=(cols // step,),
            in_specs=[
                pl.BlockSpec((rows, cols), lambda g, s: (0, 0)),
                pl.BlockSpec((rows, HALO), lambda g, s: (0, 0)),
                pl.BlockSpec((pl.Element(rows), pl.Element(cols)), lambda g, s: (pl.multiple_of(s[1], BLOCK), 0)),
                band_rows,
                band_rows,
                here,
            ],
            out_specs=here,
            scratch_shapes=[pltpu.VMEM((rows, cols + 2 * HALO), jnp.bfloat16)] * 2,
        ),
        input_output_aliases={6: 0},
        compiler_params=pltpu.CompilerParams(vmem_limit_bytes=VMEM),
        cost_estimate=SHORT,
        name="right_part",
    )(scalars, pair, strip, covariance, high, low, total)


def send(value, pairs, cols):
    return lax.ppermute(value, ("row", "col"), [(a * cols + b, c * cols + d) for (a, b), (c, d) in pairs])


def cols_route(hop, devices, ratio):
    return [
        ((r, c), (r, ((c // ratio) ^ hop) * ratio + c % ratio))
        for r, c in devices
        if ((c // ratio) ^ r) & (2 * hop - 1) == 0
    ]


def cut(total):
    first = total * 5 // 16 // BLOCK * BLOCK
    sizes = [first, first]
    left = total - 2 * first
    while left > BLOCK:
        sizes.append(-(-left // (2 * BLOCK)) * BLOCK)
        left -= sizes[-1]
    return sizes + [left] * (left > 0)


def rows_kernel(first, rows, out):
    out[...] = rows[...]


def rows_of(covariance, first, size):
    cols = covariance.shape[1]
    step = size // 2 if size % (16 * BLOCK // 8) == 0 else size
    return pl.pallas_call(
        rows_kernel,
        out_shape=jax.ShapeDtypeStruct((size, cols), covariance.dtype),
        grid_spec=pltpu.PrefetchScalarGridSpec(
            num_scalar_prefetch=1,
            grid=(size // step,),
            in_specs=[pl.BlockSpec((pl.Element(step), pl.Element(cols)), lambda j, s: (pl.multiple_of(s[0] + j * step, 8), 0))],
            out_specs=pl.BlockSpec((step, cols), lambda j, s: (j, 0)),
        ),
        cost_estimate=SHORT,
        name="rows_of",
    )(jnp.asarray(first, jnp.int32).reshape(1), covariance)


def packed_kernel(first, upper, lower, out):
    across = lax.broadcasted_iota(jnp.int32, (BLOCK, BLOCK), 1)
    down = lax.broadcasted_iota(jnp.int32, (BLOCK, BLOCK), 0)
    out[0] = jnp.where(across > down, upper[...], jnp.where(across < down, lower[...], 0.0))


def packed_diagonal(covariance, first, count):
    half = count // 2
    return pl.pallas_call(
        packed_kernel,
        out_shape=jax.ShapeDtypeStruct((half, BLOCK, BLOCK), jnp.float32),
        grid_spec=pltpu.PrefetchScalarGridSpec(
            num_scalar_prefetch=1,
            grid=(half,),
            in_specs=[
                pl.BlockSpec((BLOCK, BLOCK), lambda j, s: (s[0] + j, j)),
                pl.BlockSpec((BLOCK, BLOCK), lambda j, s: (s[0] + half + j, half + j)),
            ],
            out_specs=pl.BlockSpec((1, BLOCK, BLOCK), lambda j, s: (j, 0, 0)),
        ),
        cost_estimate=SHORT,
        name="packed_diagonal",
    )(first.reshape(1).astype(jnp.int32), covariance, covariance)


def gate_kernel(*refs):
    pass


def gate(*arrays, cost=SHORT):
    shapes = tuple(jax.ShapeDtypeStruct(array.shape, array.dtype) for array in arrays)
    anywhere = [pl.BlockSpec(memory_space=pl.ANY)] * len(arrays)
    return pl.pallas_call(
        gate_kernel,
        out_shape=shapes,
        in_specs=anywhere,
        out_specs=tuple(anywhere),
        input_output_aliases={j: j for j in range(len(arrays))},
        cost_estimate=cost,
        name="gate",
    )(*arrays)


def paired_step(covariance, couplings, block_columns, onsite):
    tile_rows, tile_cols = covariance.shape
    row_blocks, col_blocks = tile_rows // BLOCK, tile_cols // BLOCK
    total_blocks, stored = block_columns.shape
    mesh_rows, mesh_cols = lax.axis_size("row"), lax.axis_size("col")
    ratio = tile_rows // tile_cols
    row, col = lax.axis_index("row"), lax.axis_index("col")
    odd, up = col % 2, row % 2
    first_row, first_col = row * row_blocks, col * col_blocks
    offset = jnp.clip(first_col - first_row, 0, row_blocks - col_blocks)
    devices = [(r, c) for r in range(mesh_rows) for c in range(mesh_cols)]
    partners = [((r, c), (r, c ^ 1)) for r, c in devices]
    next_pairs = [((r, c), (r, (c + (2 if c % 2 == 0 else -2)) % mesh_cols)) for r, c in devices]
    inner_route = [((r, c), (r ^ 1, c)) for r, c in devices]
    outer_route = [((r, c), ((r + (-1 if r % 2 == 0 else 1)) % mesh_rows, c)) for r, c in devices]
    beside = 0
    sizes = cut(tile_rows - beside)
    firsts = [sum(sizes[:j]) for j in range(len(sizes))]
    chunks = {j: rows_of(covariance, firsts[j], sizes[j]) for j in range(len(sizes))}
    pairs, strips = {}, {}

    def move(value, route):
        return send(value, route, mesh_cols)

    def exchange(*numbers):
        for j in numbers:
            if j < len(sizes):
                pairs[j] = move(chunks[j], partners)

    def hand_strip_on(j):
        strip = lax.dynamic_slice_in_dim(pairs[j], (1 - odd) * (tile_cols - HALO), HALO, 1)
        strips[j] = move(strip, next_pairs)

    def add_right(total, j):
        first = jnp.int32(firsts[j])
        return right_part(first, odd, pairs[j], strips[j], covariance, col_high, col_low, total)

    diagonal = packed_diagonal(covariance, offset, col_blocks)
    other = move(diagonal, [((r, c), (r, c ^ 1)) for r, c in devices if c // 2 == r])
    far = tile_rows - HALO
    outer = move(rows_of(covariance, up * far, HALO), outer_route)
    other, chunks[0] = gate(other, chunks[0])
    exchange(0)
    inner = move(rows_of(covariance, (1 - up) * far, HALO), inner_route)
    both = jnp.where(odd == 0, jnp.stack([diagonal, other]), jnp.stack([other, diagonal]))
    both = both.reshape(-1, BLOCK, BLOCK)
    across, hop = (col // ratio) ^ row, mesh_cols // ratio // 2
    while hop:
        (moved,) = gate(move(both, cols_route(hop, devices, ratio)))
        both = jnp.where(across & (2 * hop - 1) == hop, moved, both)
        hop //= 2
    zero = jnp.int32(0)
    half = col_blocks // 2
    blocks = couplings.reshape(-1, BLOCK, BLOCK)
    columns = lax.dynamic_slice_in_dim(block_columns, first_row, row_blocks, 0)
    row_gains = lax.dynamic_slice_in_dim(onsite, first_row, row_blocks, 0)
    row_high, row_low = band([blocks], zero, zero, [], zero, half, columns, first_row, total_blocks, row_gains)
    row_high, row_low = add_onsite(row_high, row_low, both, half, row_gains)
    count = col_blocks * stored
    own_blocks = lax.dynamic_slice_in_dim(blocks, offset * stored, count, 0)
    held = {0: jnp.concatenate([own_blocks, diagonal], axis=0)}

    def hand_on(place):
        low = place & -place
        route = [((r, c), (r ^ low, c)) for r, c in devices if r ^ (c // ratio) == place ^ low]
        held[place] = move(held[place ^ low], route)

    places = sorted(range(1, mesh_rows), key=lambda place: (bin(place).count("1"), -place))
    nearest = [place for place in places if place & (place - 1) == 0]

    pairs[0], outer = gate(pairs[0], outer, cost=LONG)
    pairs[0], outer, inner, row_high, held[0], chunks[1], chunks[2], chunks[3] = gate(
        pairs[0], outer, inner, row_high, held[0], chunks[1], chunks[2], chunks[3]
    )
    exchange(1)
    for place in nearest:
        hand_on(place)
    hand_strip_on(0)
    total = left_part(up, inner, covariance, outer, row_high, row_low)

    for place in nearest[:-1]:
        (held[place],) = gate(held[place], cost=SOME)
    (pairs[1],) = gate(pairs[1], cost=LONG)
    pairs[1], strips[0], total, *got = gate(
        pairs[1], strips[0], total, *(held[place] for place in nearest)
    )
    held.update(zip(nearest, got))
    for place in places[len(nearest) :]:
        hand_on(place)
    exchange(2, 3)
    hand_strip_on(1)
    sources = [held[place] for place in range(mesh_rows)]
    columns = lax.dynamic_slice_in_dim(block_columns, first_col, col_blocks, 0)
    gains = lax.dynamic_slice_in_dim(onsite, first_col, col_blocks, 0)
    col_high, col_low = band(
        sources, row ^ (col // ratio), zero, sources, jnp.int32(count), half, columns, first_col, total_blocks, gains
    )
    total = add_right(total, 0)
    for j in range(2, len(sizes)):
        if j + 2 < len(sizes):
            pairs[j], total, chunks[j + 2] = gate(pairs[j], total, chunks[j + 2])
        else:
            pairs[j], total = gate(pairs[j], total)
        hand_strip_on(j)
        exchange(j + 2)
        total = add_right(total, j - 1)
    return add_right(total, len(sizes) - 1)


def power_of_two(number):
    return number & (number - 1) == 0


def on_device(covariance, couplings, block_columns, onsite):
    tile_rows, tile_cols = covariance.shape
    mesh_rows, mesh_cols = lax.axis_size("row"), lax.axis_size("col")
    fits = (
        tile_cols >= HALO
        and tile_cols % (GROUP * BLOCK) == 0
        and tile_rows == 2 * tile_cols
        and mesh_cols == 2 * mesh_rows
        and mesh_rows > 2
        and power_of_two(mesh_rows)
        and block_columns.shape[0] >= 2 * REACH + 2
    )
    step = paired_step if fits else general_step
    return step(covariance, couplings, block_columns, onsite)


def solution(mesh):
    return jax.shard_map(
        on_device,
        mesh=mesh,
        in_specs=(P("row", "col"), P("row", None, None, None), P(), P()),
        out_specs=P("row", "col"),
        check_vma=False,
    )
```

```python
import functools

import jax
import jax.numpy as jnp
from jax import lax
from jax.experimental import pallas as pl
from jax.experimental.pallas import tpu as pltpu
from jax.sharding import PartitionSpec as P

BLOCK = 128
REACH = 5


step_size = 0.25


def from_root(block, axis, holder):
    block = jnp.where(lax.axis_index(axis) == holder, block, jnp.zeros_like(block))
    return lax.psum(block, axis)


def shifted(block, axis, distance):
    devices = range(lax.axis_size(axis))
    route = [((i - distance) % len(devices), i) for i in devices]
    return lax.ppermute(block, axis, route)


def relative_positions(columns, first_block, count, total_blocks):
    own_ids = first_block + jnp.arange(count, dtype=jnp.int32)
    relative = (columns - own_ids[:, None] + total_blocks // 2) % total_blocks - total_blocks // 2
    return jnp.arange(count, dtype=jnp.int32)[:, None] + relative + REACH


def general_step(covariance, couplings, block_columns, onsite):
    tile_rows, tile_cols = covariance.shape
    row_blocks = tile_rows // BLOCK
    col_blocks = tile_cols // BLOCK
    total_blocks = block_columns.shape[0]
    reach_cells = REACH * BLOCK
    row_hops = -(-reach_cells // tile_rows)
    col_hops = -(-reach_cells // tile_cols)
    first_row = lax.axis_index("row") * row_blocks
    first_col = lax.axis_index("col") * col_blocks
    own_offset = jnp.clip(first_col - first_row, 0, row_blocks - col_blocks)
    col_root = first_col // row_blocks
    own_couplings = lax.dynamic_slice_in_dim(couplings, own_offset, col_blocks, 0)
    col_couplings = from_root(own_couplings, "row", col_root)
    row_columns = lax.dynamic_slice_in_dim(block_columns, first_row, row_blocks, 0)
    col_columns = lax.dynamic_slice_in_dim(block_columns, first_col, col_blocks, 0)
    row_positions = relative_positions(row_columns, first_row, row_blocks, total_blocks)
    col_positions = relative_positions(col_columns, first_col, col_blocks, total_blocks)
    row_gains = lax.dynamic_slice_in_dim(onsite, first_row, row_blocks, 0)
    col_gains = lax.dynamic_slice_in_dim(onsite, first_col, col_blocks, 0)
    middle = covariance
    shaped = middle.reshape(row_blocks, BLOCK, col_blocks, BLOCK)
    picked = lax.dynamic_slice_in_dim(shaped, own_offset, col_blocks, 0)
    indices = jnp.arange(col_blocks, dtype=jnp.int32)
    local_diagonal = picked[indices, :, indices, :]
    received = []
    for root_part in range(row_blocks // col_blocks):
        received.append(from_root(local_diagonal, "col", first_row // col_blocks + root_part))
    row_diagonal = jnp.concatenate(received, axis=0)
    lower_parts = []
    upper_parts = []
    for distance in range(1, row_hops + 1):
        needed = min(tile_rows, reach_cells - (distance - 1) * tile_rows)
        to_upper = middle[tile_rows - needed :]
        to_lower = middle[:needed]
        from_lower = shifted(to_upper, "row", distance)
        from_upper = shifted(to_lower, "row", -distance)
        lower_parts.insert(0, from_lower)
        upper_parts.append(from_upper)
    extended_rows = jnp.concatenate(lower_parts + [middle] + upper_parts, axis=0).reshape(
        -1, BLOCK, tile_cols
    )
    picked_rows = jnp.take(extended_rows, row_positions, axis=0)
    left_part = jnp.einsum(
        "ikab,ikbn->ian", couplings, picked_rows, precision=lax.Precision.HIGHEST
    )
    left_part = left_part + jnp.einsum(
        "iab,ibn->ian",
        row_diagonal * row_gains[:, None, None],
        middle.reshape(row_blocks, BLOCK, tile_cols),
        precision=lax.Precision.HIGHEST,
    )
    left_part = left_part.reshape(tile_rows, tile_cols)
    col_diagonal = from_root(local_diagonal, "row", col_root)
    left_parts = []
    right_parts = []
    for distance in range(1, col_hops + 1):
        needed = min(tile_cols, reach_cells - (distance - 1) * tile_cols)
        to_right = middle[:, tile_cols - needed :]
        to_left = middle[:, :needed]
        from_left = shifted(to_right, "col", distance)
        from_right = shifted(to_left, "col", -distance)
        left_parts.insert(0, from_left)
        right_parts.append(from_right)
    extended_cols = jnp.concatenate(left_parts + [middle] + right_parts, axis=1).reshape(
        tile_rows, -1, BLOCK
    )
    picked_cols = jnp.take(extended_cols, col_positions, axis=1)
    right_part = jnp.einsum(
        "nikb,ikab->nia", picked_cols, col_couplings, precision=lax.Precision.HIGHEST
    )
    right_part = right_part + jnp.einsum(
        "nib,iab->nia",
        middle.reshape(tile_rows, col_blocks, BLOCK),
        col_diagonal * col_gains[:, None, None],
        precision=lax.Precision.HIGHEST,
    )
    right_part = right_part.reshape(tile_rows, tile_cols)
    return covariance + step_size * (left_part + right_part)


GROUP = 2
WINDOW = (GROUP + 2 * REACH) * BLOCK
HALO = REACH * BLOCK
VMEM = 56 * 1024 * 1024
SHORT = pl.CostEstimate(flops=1, bytes_accessed=1, transcendentals=0)
SOME = pl.CostEstimate(flops=10**10, bytes_accessed=4 * 10**7, transcendentals=0)
LONG = pl.CostEstimate(flops=4 * 10**11, bytes_accessed=16 * 10**8, transcendentals=0)


def halves(value):
    high = value.astype(jnp.bfloat16)
    return high, (value - high.astype(jnp.float32)).astype(jnp.bfloat16)


def product(a_high, a_low, b_high, b_low, contract_b=0):
    dims = (((1,), (contract_b,)), ((), ()))
    dot = functools.partial(lax.dot_general, dimension_numbers=dims, preferred_element_type=jnp.float32)
    return dot(a_high, b_high) + (dot(a_high, b_low) + dot(a_low, b_high))


def band_kernel(places, gains, scalars, *refs, sources, half):
    blocks, diagonals, (high, low, whole) = refs[:sources], refs[sources:-3], refs[-3:]
    i = pl.program_id(0)
    whole[...] = jnp.zeros_like(whole)
    down = lax.broadcasted_iota(jnp.int32, (BLOCK, BLOCK), 0)
    across = lax.broadcasted_iota(jnp.int32, (BLOCK, BLOCK), 1)
    beyond = jnp.where(i % (2 * half) < half, across - down, down - across)
    own = pl.multiple_of((REACH + i % GROUP) * BLOCK, BLOCK)
    for source in range(sources):

        @pl.when(scalars[0] == source)
        def _():
            for k in range(blocks[source].shape[0]):
                place = pl.multiple_of(places[i, k] * BLOCK, BLOCK)
                whole[:, pl.ds(place, BLOCK)] = blocks[source][k]
            if diagonals:
                part = jnp.where(beyond > 0, diagonals[source][0], 0.0)
                whole[:, pl.ds(own, BLOCK)] += gains[i] * (part - part.T)

    high[...], low[...] = halves(whole[...])


def band(sources, choice, offset, diagonals, diagonal_offset, half, columns, first_block, total_blocks, gains):
    count, stored = columns.shape
    own_ids = first_block + jnp.arange(count, dtype=jnp.int32)
    relative = (columns - own_ids[:, None] + total_blocks // 2) % total_blocks - total_blocks // 2
    places = relative + REACH + (jnp.arange(count, dtype=jnp.int32) % GROUP)[:, None]
    shape = jax.ShapeDtypeStruct((count * BLOCK, WINDOW), jnp.bfloat16)

    def blocks_of(source):
        def index(i, places, gains, scalars):
            return (jnp.where(scalars[0] == source, scalars[1] + i, 0), 0, 0)

        return pl.BlockSpec((stored, BLOCK, BLOCK), index)

    def diagonal_of(source):
        def index(i, places, gains, scalars):
            return (jnp.where(scalars[0] == source, scalars[2] + i // (2 * half) * half + i % half, 0), 0, 0)

        return pl.BlockSpec((1, BLOCK, BLOCK), index)

    return pl.pallas_call(
        functools.partial(band_kernel, sources=len(sources), half=half),
        out_shape=(shape, shape),
        grid_spec=pltpu.PrefetchScalarGridSpec(
            num_scalar_prefetch=3,
            grid=(count,),
            in_specs=[blocks_of(j) for j in range(len(sources))] + [diagonal_of(j) for j in range(len(diagonals))],
            out_specs=[pl.BlockSpec((BLOCK, WINDOW), lambda i, *_: (i, 0))] * 2,
            scratch_shapes=[pltpu.VMEM((BLOCK, WINDOW), jnp.float32)],
        ),
        compiler_params=pltpu.CompilerParams(vmem_limit_bytes=VMEM),
        cost_estimate=SHORT,
        name="band",
    )(places, gains, jnp.stack([choice, offset, diagonal_offset]).astype(jnp.int32), *sources, *diagonals)


def onsite_kernel(gains, *refs, half):
    diagonals, (high, low, new_high, new_low) = refs[:GROUP], refs[GROUP:]
    g = pl.program_id(0)
    down = lax.broadcasted_iota(jnp.int32, (BLOCK, BLOCK), 0)
    across = lax.broadcasted_iota(jnp.int32, (BLOCK, BLOCK), 1)
    new_high[...], new_low[...] = high[...], low[...]
    for b, diagonal in enumerate(diagonals):
        i = g * GROUP + b
        here = slice(b * BLOCK, (b + 1) * BLOCK)
        beyond = jnp.where(i % (2 * half) < half, across - down, down - across)
        part = jnp.where(beyond > 0, diagonal[0], 0.0)
        value = high[here, here].astype(jnp.float32) + low[here, here].astype(jnp.float32)
        new_high[here, here], new_low[here, here] = halves(value + gains[i] * (part - part.T))


def add_onsite(high, low, diagonals, half, gains):
    step = GROUP * BLOCK
    own = pl.BlockSpec((pl.Element(step), pl.Element(step)), lambda g, gains: (g * step, HALO))
    shape = jax.ShapeDtypeStruct(high.shape, high.dtype)

    def diagonal_of(b):
        def index(g, gains):
            i = g * GROUP + b
            return (i // (2 * half) * half + i % half, 0, 0)

        return pl.BlockSpec((1, BLOCK, BLOCK), index)

    return pl.pallas_call(
        functools.partial(onsite_kernel, half=half),
        out_shape=(shape, shape),
        grid_spec=pltpu.PrefetchScalarGridSpec(
            num_scalar_prefetch=1,
            grid=(high.shape[0] // step,),
            in_specs=[diagonal_of(b) for b in range(GROUP)] + [own, own],
            out_specs=[own, own],
        ),
        input_output_aliases={1 + GROUP: 0, 2 + GROUP: 1},
        compiler_params=pltpu.CompilerParams(vmem_limit_bytes=VMEM),
        cost_estimate=SHORT,
        name="add_onsite",
    )(gains, *([diagonals] * GROUP), high, low)


def left_kernel(up, inner, own, outer, high, low, out, ext_high, ext_low):
    rows = own.shape[0]
    top = jnp.where(up[0] == 0, outer[...], inner[...])
    bottom = jnp.where(up[0] == 0, inner[...], outer[...])
    for start, part in ((0, top), (HALO, own[...]), (HALO + rows, bottom)):
        size = part.shape[0]
        ext_high[start : start + size], ext_low[start : start + size] = halves(part)
    step = GROUP * BLOCK
    for g in range(rows // step):
        here, window = slice(g * step, (g + 1) * step), slice(g * step, g * step + WINDOW)
        value = product(high[here], low[here], ext_high[window], ext_low[window])
        out[here] = own[here] + step_size * value


def left_part(up, inner, covariance, outer, high, low, slab=2 * BLOCK):
    rows, cols = covariance.shape
    whole = pl.BlockSpec((rows, WINDOW), lambda j, s: (0, 0), pipeline_mode=pl.Buffered(1))
    beyond = pl.BlockSpec((HALO, slab), lambda j, s: (0, j))
    here = pl.BlockSpec((rows, slab), lambda j, s: (0, j))
    return pl.pallas_call(
        left_kernel,
        out_shape=jax.ShapeDtypeStruct((rows, cols), jnp.float32),
        grid_spec=pltpu.PrefetchScalarGridSpec(
            num_scalar_prefetch=1,
            grid=(cols // slab,),
            in_specs=[beyond, here, beyond, whole, whole],
            out_specs=here,
            scratch_shapes=[pltpu.VMEM((rows + 2 * HALO, slab), jnp.bfloat16)] * 2,
        ),
        compiler_params=pltpu.CompilerParams(vmem_limit_bytes=VMEM),
        cost_estimate=SHORT,
        name="left_part",
    )(up.reshape(1).astype(jnp.int32), inner, covariance, outer, high, low)


def right_kernel(scalars, pair, strip, own, high, low, total, out, ext_high, ext_low):
    cols = own.shape[1]

    def put(start, value):
        end = start + value.shape[1]
        ext_high[:, start:end], ext_low[:, start:end] = halves(value)

    g = pl.program_id(0)

    @pl.when(g == 0)
    def _():
        put(HALO, own[...])

    @pl.when((g == 0) & (scalars[0] == 0))
    def _():
        put(0, strip[...])
        put(HALO + cols, pair[:, :HALO])

    @pl.when((g == 0) & (scalars[0] == 1))
    def _():
        put(0, pair[:, cols - HALO :])
        put(HALO + cols, strip[...])

    window = pl.ds(pl.multiple_of(g * (GROUP * BLOCK), GROUP * BLOCK), WINDOW)
    value = product(ext_high[:, window], ext_low[:, window], high[...], low[...], 1)
    out[...] = total[...] + step_size * value


def right_part(first, odd, pair, strip, covariance, high, low, total):
    rows, cols = pair.shape
    step = GROUP * BLOCK
    scalars = jnp.stack([odd, first]).astype(jnp.int32)
    band_rows = pl.BlockSpec((step, WINDOW), lambda g, s: (g, 0))
    here = pl.BlockSpec((pl.Element(rows), pl.Element(step)), lambda g, s: (pl.multiple_of(s[1], BLOCK), g * step))
    return pl.pallas_call(
        right_kernel,
        out_shape=jax.ShapeDtypeStruct(total.shape, jnp.float32),
        grid_spec=pltpu.PrefetchScalarGridSpec(
            num_scalar_prefetch=1,
            grid=(cols // step,),
            in_specs=[
                pl.BlockSpec((rows, cols), lambda g, s: (0, 0)),
                pl.BlockSpec((rows, HALO), lambda g, s: (0, 0)),
                pl.BlockSpec((pl.Element(rows), pl.Element(cols)), lambda g, s: (pl.multiple_of(s[1], BLOCK), 0)),
                band_rows,
                band_rows,
                here,
            ],
            out_specs=here,
            scratch_shapes=[pltpu.VMEM((rows, cols + 2 * HALO), jnp.bfloat16)] * 2,
        ),
        input_output_aliases={6: 0},
        compiler_params=pltpu.CompilerParams(vmem_limit_bytes=VMEM),
        cost_estimate=SHORT,
        name="right_part",
    )(scalars, pair, strip, covariance, high, low, total)


def send(value, pairs, cols):
    return lax.ppermute(value, ("row", "col"), [(a * cols + b, c * cols + d) for (a, b), (c, d) in pairs])


def cols_route(hop, devices, ratio):
    return [
        ((r, c), (r, ((c // ratio) ^ hop) * ratio + c % ratio))
        for r, c in devices
        if ((c // ratio) ^ r) & (2 * hop - 1) == 0
    ]


def cut(total):
    first = total * 5 // 16 // BLOCK * BLOCK
    sizes = [first, first]
    left = total - 2 * first
    while left:
        sizes.append(min(left, 2 * BLOCK))
        left -= sizes[-1]
    return sizes


def rows_kernel(first, rows, out):
    out[...] = rows[...]


def rows_of(covariance, first, size):
    cols = covariance.shape[1]
    step = size // 2 if size % (16 * BLOCK // 8) == 0 else size
    return pl.pallas_call(
        rows_kernel,
        out_shape=jax.ShapeDtypeStruct((size, cols), covariance.dtype),
        grid_spec=pltpu.PrefetchScalarGridSpec(
            num_scalar_prefetch=1,
            grid=(size // step,),
            in_specs=[pl.BlockSpec((pl.Element(step), pl.Element(cols)), lambda j, s: (pl.multiple_of(s[0] + j * step, 8), 0))],
            out_specs=pl.BlockSpec((step, cols), lambda j, s: (j, 0)),
        ),
        cost_estimate=SHORT,
        name="rows_of",
    )(jnp.asarray(first, jnp.int32).reshape(1), covariance)


def packed_kernel(first, upper, lower, out):
    across = lax.broadcasted_iota(jnp.int32, (BLOCK, BLOCK), 1)
    down = lax.broadcasted_iota(jnp.int32, (BLOCK, BLOCK), 0)
    out[0] = jnp.where(across > down, upper[...], jnp.where(across < down, lower[...], 0.0))


def packed_diagonal(covariance, first, count):
    half = count // 2
    return pl.pallas_call(
        packed_kernel,
        out_shape=jax.ShapeDtypeStruct((half, BLOCK, BLOCK), jnp.float32),
        grid_spec=pltpu.PrefetchScalarGridSpec(
            num_scalar_prefetch=1,
            grid=(half,),
            in_specs=[
                pl.BlockSpec((BLOCK, BLOCK), lambda j, s: (s[0] + j, j)),
                pl.BlockSpec((BLOCK, BLOCK), lambda j, s: (s[0] + half + j, half + j)),
            ],
            out_specs=pl.BlockSpec((1, BLOCK, BLOCK), lambda j, s: (j, 0, 0)),
        ),
        cost_estimate=SHORT,
        name="packed_diagonal",
    )(first.reshape(1).astype(jnp.int32), covariance, covariance)


def gate_kernel(*refs):
    pass


def gate(*arrays, cost=SHORT):
    shapes = tuple(jax.ShapeDtypeStruct(array.shape, array.dtype) for array in arrays)
    anywhere = [pl.BlockSpec(memory_space=pl.ANY)] * len(arrays)
    return pl.pallas_call(
        gate_kernel,
        out_shape=shapes,
        in_specs=anywhere,
        out_specs=tuple(anywhere),
        input_output_aliases={j: j for j in range(len(arrays))},
        cost_estimate=cost,
        name="gate",
    )(*arrays)


def paired_step(covariance, couplings, block_columns, onsite):
    tile_rows, tile_cols = covariance.shape
    row_blocks, col_blocks = tile_rows // BLOCK, tile_cols // BLOCK
    total_blocks, stored = block_columns.shape
    mesh_rows, mesh_cols = lax.axis_size("row"), lax.axis_size("col")
    ratio = tile_rows // tile_cols
    row, col = lax.axis_index("row"), lax.axis_index("col")
    odd, up = col % 2, row % 2
    first_row, first_col = row * row_blocks, col * col_blocks
    offset = jnp.clip(first_col - first_row, 0, row_blocks - col_blocks)
    devices = [(r, c) for r in range(mesh_rows) for c in range(mesh_cols)]
    partners = [((r, c), (r, c ^ 1)) for r, c in devices]
    next_pairs = [((r, c), (r, (c + (2 if c % 2 == 0 else -2)) % mesh_cols)) for r, c in devices]
    inner_route = [((r, c), (r ^ 1, c)) for r, c in devices]
    outer_route = [((r, c), ((r + (-1 if r % 2 == 0 else 1)) % mesh_rows, c)) for r, c in devices]
    beside = 0
    sizes = cut(tile_rows - beside)
    firsts = [sum(sizes[:j]) for j in range(len(sizes))]
    chunks = {j: rows_of(covariance, firsts[j], sizes[j]) for j in range(len(sizes))}
    pairs, strips = {}, {}

    def move(value, route):
        return send(value, route, mesh_cols)

    def exchange(*numbers):
        for j in numbers:
            if j < len(sizes):
                pairs[j] = move(chunks[j], partners)

    def hand_strip_on(j):
        strip = lax.dynamic_slice_in_dim(pairs[j], (1 - odd) * (tile_cols - HALO), HALO, 1)
        strips[j] = move(strip, next_pairs)

    def add_right(total, j):
        first = jnp.int32(firsts[j])
        return right_part(first, odd, pairs[j], strips[j], covariance, col_high, col_low, total)

    diagonal = packed_diagonal(covariance, offset, col_blocks)
    other = move(diagonal, [((r, c), (r, c ^ 1)) for r, c in devices if c // 2 == r])
    far = tile_rows - HALO
    outer = move(rows_of(covariance, up * far, HALO), outer_route)
    other, chunks[0] = gate(other, chunks[0])
    exchange(0)
    inner = move(rows_of(covariance, (1 - up) * far, HALO), inner_route)
    both = jnp.where(odd == 0, jnp.stack([diagonal, other]), jnp.stack([other, diagonal]))
    both = both.reshape(-1, BLOCK, BLOCK)
    across, hop = (col // ratio) ^ row, mesh_cols // ratio // 2
    while hop:
        (moved,) = gate(move(both, cols_route(hop, devices, ratio)))
        both = jnp.where(across & (2 * hop - 1) == hop, moved, both)
        hop //= 2
    zero = jnp.int32(0)
    half = col_blocks // 2
    blocks = couplings.reshape(-1, BLOCK, BLOCK)
    columns = lax.dynamic_slice_in_dim(block_columns, first_row, row_blocks, 0)
    row_gains = lax.dynamic_slice_in_dim(onsite, first_row, row_blocks, 0)
    row_high, row_low = band([blocks], zero, zero, [], zero, half, columns, first_row, total_blocks, row_gains)
    row_high, row_low = add_onsite(row_high, row_low, both, half, row_gains)
    count = col_blocks * stored
    own_blocks = lax.dynamic_slice_in_dim(blocks, offset * stored, count, 0)
    held = {0: jnp.concatenate([own_blocks, diagonal], axis=0)}

    def hand_on(place):
        low = place & -place
        route = [((r, c), (r ^ low, c)) for r, c in devices if r ^ (c // ratio) == place ^ low]
        held[place] = move(held[place ^ low], route)

    places = sorted(range(1, mesh_rows), key=lambda place: (bin(place).count("1"), -place))
    nearest = [place for place in places if place & (place - 1) == 0]

    pairs[0], outer = gate(pairs[0], outer, cost=LONG)
    pairs[0], outer, inner, row_high, held[0], chunks[1], chunks[2], chunks[3] = gate(
        pairs[0], outer, inner, row_high, held[0], chunks[1], chunks[2], chunks[3]
    )
    exchange(1)
    for place in nearest:
        hand_on(place)
    hand_strip_on(0)
    total = left_part(up, inner, covariance, outer, row_high, row_low)

    for place in nearest[:-1]:
        (held[place],) = gate(held[place], cost=SOME)
    (pairs[1],) = gate(pairs[1], cost=LONG)
    pairs[1], strips[0], total, *got = gate(
        pairs[1], strips[0], total, *(held[place] for place in nearest)
    )
    held.update(zip(nearest, got))
    for place in places[len(nearest) :]:
        hand_on(place)
    exchange(2, 3)
    hand_strip_on(1)
    sources = [held[place] for place in range(mesh_rows)]
    columns = lax.dynamic_slice_in_dim(block_columns, first_col, col_blocks, 0)
    gains = lax.dynamic_slice_in_dim(onsite, first_col, col_blocks, 0)
    col_high, col_low = band(
        sources, row ^ (col // ratio), zero, sources, jnp.int32(count), half, columns, first_col, total_blocks, gains
    )
    total = add_right(total, 0)
    for j in range(2, len(sizes)):
        if j + 2 < len(sizes):
            pairs[j], total, chunks[j + 2] = gate(pairs[j], total, chunks[j + 2])
        else:
            pairs[j], total = gate(pairs[j], total)
        hand_strip_on(j)
        exchange(j + 2)
        total = add_right(total, j - 1)
    return add_right(total, len(sizes) - 1)


def power_of_two(number):
    return number & (number - 1) == 0


def on_device(covariance, couplings, block_columns, onsite):
    tile_rows, tile_cols = covariance.shape
    mesh_rows, mesh_cols = lax.axis_size("row"), lax.axis_size("col")
    fits = (
        tile_cols >= HALO
        and tile_cols % (GROUP * BLOCK) == 0
        and tile_rows == 2 * tile_cols
        and mesh_cols == 2 * mesh_rows
        and mesh_rows > 2
        and power_of_two(mesh_rows)
        and block_columns.shape[0] >= 2 * REACH + 2
    )
    step = paired_step if fits else general_step
    return step(covariance, couplings, block_columns, onsite)


def solution(mesh):
    return jax.shard_map(
        on_device,
        mesh=mesh,
        in_specs=(P("row", "col"), P("row", None, None, None), P(), P()),
        out_specs=P("row", "col"),
        check_vma=False,
    )
```

```python
import functools

import jax
import jax.numpy as jnp
from jax import lax
from jax.experimental import pallas as pl
from jax.experimental.pallas import tpu as pltpu
from jax.sharding import PartitionSpec as P

BLOCK = 128
REACH = 5


step_size = 0.25


def from_root(block, axis, holder):
    block = jnp.where(lax.axis_index(axis) == holder, block, jnp.zeros_like(block))
    return lax.psum(block, axis)


def shifted(block, axis, distance):
    devices = range(lax.axis_size(axis))
    route = [((i - distance) % len(devices), i) for i in devices]
    return lax.ppermute(block, axis, route)


def relative_positions(columns, first_block, count, total_blocks):
    own_ids = first_block + jnp.arange(count, dtype=jnp.int32)
    relative = (columns - own_ids[:, None] + total_blocks // 2) % total_blocks - total_blocks // 2
    return jnp.arange(count, dtype=jnp.int32)[:, None] + relative + REACH


def general_step(covariance, couplings, block_columns, onsite):
    tile_rows, tile_cols = covariance.shape
    row_blocks = tile_rows // BLOCK
    col_blocks = tile_cols // BLOCK
    total_blocks = block_columns.shape[0]
    reach_cells = REACH * BLOCK
    row_hops = -(-reach_cells // tile_rows)
    col_hops = -(-reach_cells // tile_cols)
    first_row = lax.axis_index("row") * row_blocks
    first_col = lax.axis_index("col") * col_blocks
    own_offset = jnp.clip(first_col - first_row, 0, row_blocks - col_blocks)
    col_root = first_col // row_blocks
    own_couplings = lax.dynamic_slice_in_dim(couplings, own_offset, col_blocks, 0)
    col_couplings = from_root(own_couplings, "row", col_root)
    row_columns = lax.dynamic_slice_in_dim(block_columns, first_row, row_blocks, 0)
    col_columns = lax.dynamic_slice_in_dim(block_columns, first_col, col_blocks, 0)
    row_positions = relative_positions(row_columns, first_row, row_blocks, total_blocks)
    col_positions = relative_positions(col_columns, first_col, col_blocks, total_blocks)
    row_gains = lax.dynamic_slice_in_dim(onsite, first_row, row_blocks, 0)
    col_gains = lax.dynamic_slice_in_dim(onsite, first_col, col_blocks, 0)
    middle = covariance
    shaped = middle.reshape(row_blocks, BLOCK, col_blocks, BLOCK)
    picked = lax.dynamic_slice_in_dim(shaped, own_offset, col_blocks, 0)
    indices = jnp.arange(col_blocks, dtype=jnp.int32)
    local_diagonal = picked[indices, :, indices, :]
    received = []
    for root_part in range(row_blocks // col_blocks):
        received.append(from_root(local_diagonal, "col", first_row // col_blocks + root_part))
    row_diagonal = jnp.concatenate(received, axis=0)
    lower_parts = []
    upper_parts = []
    for distance in range(1, row_hops + 1):
        needed = min(tile_rows, reach_cells - (distance - 1) * tile_rows)
        to_upper = middle[tile_rows - needed :]
        to_lower = middle[:needed]
        from_lower = shifted(to_upper, "row", distance)
        from_upper = shifted(to_lower, "row", -distance)
        lower_parts.insert(0, from_lower)
        upper_parts.append(from_upper)
    extended_rows = jnp.concatenate(lower_parts + [middle] + upper_parts, axis=0).reshape(
        -1, BLOCK, tile_cols
    )
    picked_rows = jnp.take(extended_rows, row_positions, axis=0)
    left_part = jnp.einsum(
        "ikab,ikbn->ian", couplings, picked_rows, precision=lax.Precision.HIGHEST
    )
    left_part = left_part + jnp.einsum(
        "iab,ibn->ian",
        row_diagonal * row_gains[:, None, None],
        middle.reshape(row_blocks, BLOCK, tile_cols),
        precision=lax.Precision.HIGHEST,
    )
    left_part = left_part.reshape(tile_rows, tile_cols)
    col_diagonal = from_root(local_diagonal, "row", col_root)
    left_parts = []
    right_parts = []
    for distance in range(1, col_hops + 1):
        needed = min(tile_cols, reach_cells - (distance - 1) * tile_cols)
        to_right = middle[:, tile_cols - needed :]
        to_left = middle[:, :needed]
        from_left = shifted(to_right, "col", distance)
        from_right = shifted(to_left, "col", -distance)
        left_parts.insert(0, from_left)
        right_parts.append(from_right)
    extended_cols = jnp.concatenate(left_parts + [middle] + right_parts, axis=1).reshape(
        tile_rows, -1, BLOCK
    )
    picked_cols = jnp.take(extended_cols, col_positions, axis=1)
    right_part = jnp.einsum(
        "nikb,ikab->nia", picked_cols, col_couplings, precision=lax.Precision.HIGHEST
    )
    right_part = right_part + jnp.einsum(
        "nib,iab->nia",
        middle.reshape(tile_rows, col_blocks, BLOCK),
        col_diagonal * col_gains[:, None, None],
        precision=lax.Precision.HIGHEST,
    )
    right_part = right_part.reshape(tile_rows, tile_cols)
    return covariance + step_size * (left_part + right_part)


GROUP = 2
WINDOW = (GROUP + 2 * REACH) * BLOCK
HALO = REACH * BLOCK
VMEM = 56 * 1024 * 1024
SHORT = pl.CostEstimate(flops=1, bytes_accessed=1, transcendentals=0)
SOME = pl.CostEstimate(flops=10**10, bytes_accessed=4 * 10**7, transcendentals=0)
LONG = pl.CostEstimate(flops=4 * 10**11, bytes_accessed=16 * 10**8, transcendentals=0)


def halves(value):
    high = value.astype(jnp.bfloat16)
    return high, (value - high.astype(jnp.float32)).astype(jnp.bfloat16)


def product(a_high, a_low, b_high, b_low, contract_b=0):
    dims = (((1,), (contract_b,)), ((), ()))
    dot = functools.partial(lax.dot_general, dimension_numbers=dims, preferred_element_type=jnp.float32)
    return dot(a_high, b_high) + (dot(a_high, b_low) + dot(a_low, b_high))


def band_kernel(places, gains, scalars, *refs, sources, half):
    blocks, diagonals, (high, low, whole) = refs[:sources], refs[sources:-3], refs[-3:]
    i = pl.program_id(0)
    whole[...] = jnp.zeros_like(whole)
    down = lax.broadcasted_iota(jnp.int32, (BLOCK, BLOCK), 0)
    across = lax.broadcasted_iota(jnp.int32, (BLOCK, BLOCK), 1)
    beyond = jnp.where(i % (2 * half) < half, across - down, down - across)
    own = pl.multiple_of((REACH + i % GROUP) * BLOCK, BLOCK)
    for source in range(sources):

        @pl.when(scalars[0] == source)
        def _():
            for k in range(blocks[source].shape[0]):
                place = pl.multiple_of(places[i, k] * BLOCK, BLOCK)
                whole[:, pl.ds(place, BLOCK)] = blocks[source][k]
            if diagonals:
                part = jnp.where(beyond > 0, diagonals[source][0], 0.0)
                whole[:, pl.ds(own, BLOCK)] += gains[i] * (part - part.T)

    high[...], low[...] = halves(whole[...])


def band(sources, choice, offset, diagonals, diagonal_offset, half, columns, first_block, total_blocks, gains):
    count, stored = columns.shape
    own_ids = first_block + jnp.arange(count, dtype=jnp.int32)
    relative = (columns - own_ids[:, None] + total_blocks // 2) % total_blocks - total_blocks // 2
    places = relative + REACH + (jnp.arange(count, dtype=jnp.int32) % GROUP)[:, None]
    shape = jax.ShapeDtypeStruct((count * BLOCK, WINDOW), jnp.bfloat16)

    def blocks_of(source):
        def index(i, places, gains, scalars):
            return (jnp.where(scalars[0] == source, scalars[1] + i, 0), 0, 0)

        return pl.BlockSpec((stored, BLOCK, BLOCK), index)

    def diagonal_of(source):
        def index(i, places, gains, scalars):
            return (jnp.where(scalars[0] == source, scalars[2] + i // (2 * half) * half + i % half, 0), 0, 0)

        return pl.BlockSpec((1, BLOCK, BLOCK), index)

    return pl.pallas_call(
        functools.partial(band_kernel, sources=len(sources), half=half),
        out_shape=(shape, shape),
        grid_spec=pltpu.PrefetchScalarGridSpec(
            num_scalar_prefetch=3,
            grid=(count,),
            in_specs=[blocks_of(j) for j in range(len(sources))] + [diagonal_of(j) for j in range(len(diagonals))],
            out_specs=[pl.BlockSpec((BLOCK, WINDOW), lambda i, *_: (i, 0))] * 2,
            scratch_shapes=[pltpu.VMEM((BLOCK, WINDOW), jnp.float32)],
        ),
        compiler_params=pltpu.CompilerParams(vmem_limit_bytes=VMEM),
        cost_estimate=SHORT,
        name="band",
    )(places, gains, jnp.stack([choice, offset, diagonal_offset]).astype(jnp.int32), *sources, *diagonals)


def onsite_kernel(gains, *refs, half):
    diagonals, (high, low, new_high, new_low) = refs[:GROUP], refs[GROUP:]
    g = pl.program_id(0)
    down = lax.broadcasted_iota(jnp.int32, (BLOCK, BLOCK), 0)
    across = lax.broadcasted_iota(jnp.int32, (BLOCK, BLOCK), 1)
    new_high[...], new_low[...] = high[...], low[...]
    for b, diagonal in enumerate(diagonals):
        i = g * GROUP + b
        here = slice(b * BLOCK, (b + 1) * BLOCK)
        beyond = jnp.where(i % (2 * half) < half, across - down, down - across)
        part = jnp.where(beyond > 0, diagonal[0], 0.0)
        value = high[here, here].astype(jnp.float32) + low[here, here].astype(jnp.float32)
        new_high[here, here], new_low[here, here] = halves(value + gains[i] * (part - part.T))


def add_onsite(high, low, diagonals, half, gains):
    step = GROUP * BLOCK
    own = pl.BlockSpec((pl.Element(step), pl.Element(step)), lambda g, gains: (g * step, HALO))
    shape = jax.ShapeDtypeStruct(high.shape, high.dtype)

    def diagonal_of(b):
        def index(g, gains):
            i = g * GROUP + b
            return (i // (2 * half) * half + i % half, 0, 0)

        return pl.BlockSpec((1, BLOCK, BLOCK), index)

    return pl.pallas_call(
        functools.partial(onsite_kernel, half=half),
        out_shape=(shape, shape),
        grid_spec=pltpu.PrefetchScalarGridSpec(
            num_scalar_prefetch=1,
            grid=(high.shape[0] // step,),
            in_specs=[diagonal_of(b) for b in range(GROUP)] + [own, own],
            out_specs=[own, own],
        ),
        input_output_aliases={1 + GROUP: 0, 2 + GROUP: 1},
        compiler_params=pltpu.CompilerParams(vmem_limit_bytes=VMEM),
        cost_estimate=SHORT,
        name="add_onsite",
    )(gains, *([diagonals] * GROUP), high, low)


def left_kernel(up, inner, own, outer, high, low, out, ext_high, ext_low):
    rows = own.shape[0]
    top = jnp.where(up[0] == 0, outer[...], inner[...])
    bottom = jnp.where(up[0] == 0, inner[...], outer[...])
    for start, part in ((0, top), (HALO, own[...]), (HALO + rows, bottom)):
        size = part.shape[0]
        ext_high[start : start + size], ext_low[start : start + size] = halves(part)
    step = GROUP * BLOCK
    for g in range(rows // step):
        here, window = slice(g * step, (g + 1) * step), slice(g * step, g * step + WINDOW)
        value = product(high[here], low[here], ext_high[window], ext_low[window])
        out[here] = own[here] + step_size * value


def left_part(up, inner, covariance, outer, high, low, slab=2 * BLOCK):
    rows, cols = covariance.shape
    whole = pl.BlockSpec((rows, WINDOW), lambda j, s: (0, 0), pipeline_mode=pl.Buffered(1))
    beyond = pl.BlockSpec((HALO, slab), lambda j, s: (0, j))
    here = pl.BlockSpec((rows, slab), lambda j, s: (0, j))
    return pl.pallas_call(
        left_kernel,
        out_shape=jax.ShapeDtypeStruct((rows, cols), jnp.float32),
        grid_spec=pltpu.PrefetchScalarGridSpec(
            num_scalar_prefetch=1,
            grid=(cols // slab,),
            in_specs=[beyond, here, beyond, whole, whole],
            out_specs=here,
            scratch_shapes=[pltpu.VMEM((rows + 2 * HALO, slab), jnp.bfloat16)] * 2,
        ),
        compiler_params=pltpu.CompilerParams(vmem_limit_bytes=VMEM),
        cost_estimate=SHORT,
        name="left_part",
    )(up.reshape(1).astype(jnp.int32), inner, covariance, outer, high, low)


def right_kernel(scalars, pair, strip, own, high, low, total, out, ext_high, ext_low):
    cols = own.shape[1]

    def put(start, value):
        end = start + value.shape[1]
        ext_high[:, start:end], ext_low[:, start:end] = halves(value)

    g = pl.program_id(0)

    @pl.when(g == 0)
    def _():
        put(HALO, own[...])

    @pl.when((g == 0) & (scalars[0] == 0))
    def _():
        put(0, strip[...])
        put(HALO + cols, pair[:, :HALO])

    @pl.when((g == 0) & (scalars[0] == 1))
    def _():
        put(0, pair[:, cols - HALO :])
        put(HALO + cols, strip[...])

    window = pl.ds(pl.multiple_of(g * (GROUP * BLOCK), GROUP * BLOCK), WINDOW)
    value = product(ext_high[:, window], ext_low[:, window], high[...], low[...], 1)
    out[...] = total[...] + step_size * value


def right_part(first, odd, pair, strip, covariance, high, low, total):
    rows, cols = pair.shape
    step = GROUP * BLOCK
    scalars = jnp.stack([odd, first]).astype(jnp.int32)
    band_rows = pl.BlockSpec((step, WINDOW), lambda g, s: (g, 0))
    here = pl.BlockSpec((pl.Element(rows), pl.Element(step)), lambda g, s: (pl.multiple_of(s[1], BLOCK // 2), g * step))
    return pl.pallas_call(
        right_kernel,
        out_shape=jax.ShapeDtypeStruct(total.shape, jnp.float32),
        grid_spec=pltpu.PrefetchScalarGridSpec(
            num_scalar_prefetch=1,
            grid=(cols // step,),
            in_specs=[
                pl.BlockSpec((rows, cols), lambda g, s: (0, 0)),
                pl.BlockSpec((rows, HALO), lambda g, s: (0, 0)),
                pl.BlockSpec((pl.Element(rows), pl.Element(cols)), lambda g, s: (pl.multiple_of(s[1], BLOCK // 2), 0)),
                band_rows,
                band_rows,
                here,
            ],
            out_specs=here,
            scratch_shapes=[pltpu.VMEM((rows, cols + 2 * HALO), jnp.bfloat16)] * 2,
        ),
        input_output_aliases={6: 0},
        compiler_params=pltpu.CompilerParams(vmem_limit_bytes=VMEM),
        cost_estimate=SHORT,
        name="right_part",
    )(scalars, pair, strip, covariance, high, low, total)


def send(value, pairs, cols):
    return lax.ppermute(value, ("row", "col"), [(a * cols + b, c * cols + d) for (a, b), (c, d) in pairs])


def cols_route(hop, devices, ratio):
    return [
        ((r, c), (r, ((c // ratio) ^ hop) * ratio + c % ratio))
        for r, c in devices
        if ((c // ratio) ^ r) & (2 * hop - 1) == 0
    ]


def cut(total):
    first = total * 5 // 16 // BLOCK * BLOCK
    more = BLOCK // 2
    left = total - 2 * first
    third = -(-left // (2 * BLOCK)) * BLOCK
    return [first, first + more, third - more, left - third - BLOCK, BLOCK]


def rows_kernel(first, rows, out):
    out[...] = rows[...]


def rows_of(covariance, first, size):
    cols = covariance.shape[1]
    step = size // 2 if size % (16 * BLOCK // 8) == 0 else size
    return pl.pallas_call(
        rows_kernel,
        out_shape=jax.ShapeDtypeStruct((size, cols), covariance.dtype),
        grid_spec=pltpu.PrefetchScalarGridSpec(
            num_scalar_prefetch=1,
            grid=(size // step,),
            in_specs=[pl.BlockSpec((pl.Element(step), pl.Element(cols)), lambda j, s: (pl.multiple_of(s[0] + j * step, 8), 0))],
            out_specs=pl.BlockSpec((step, cols), lambda j, s: (j, 0)),
        ),
        cost_estimate=SHORT,
        name="rows_of",
    )(jnp.asarray(first, jnp.int32).reshape(1), covariance)


def packed_kernel(first, upper, lower, out):
    across = lax.broadcasted_iota(jnp.int32, (BLOCK, BLOCK), 1)
    down = lax.broadcasted_iota(jnp.int32, (BLOCK, BLOCK), 0)
    out[0] = jnp.where(across > down, upper[...], jnp.where(across < down, lower[...], 0.0))


def packed_diagonal(covariance, first, count):
    half = count // 2
    return pl.pallas_call(
        packed_kernel,
        out_shape=jax.ShapeDtypeStruct((half, BLOCK, BLOCK), jnp.float32),
        grid_spec=pltpu.PrefetchScalarGridSpec(
            num_scalar_prefetch=1,
            grid=(half,),
            in_specs=[
                pl.BlockSpec((BLOCK, BLOCK), lambda j, s: (s[0] + j, j)),
                pl.BlockSpec((BLOCK, BLOCK), lambda j, s: (s[0] + half + j, half + j)),
            ],
            out_specs=pl.BlockSpec((1, BLOCK, BLOCK), lambda j, s: (j, 0, 0)),
        ),
        cost_estimate=SHORT,
        name="packed_diagonal",
    )(first.reshape(1).astype(jnp.int32), covariance, covariance)


def gate_kernel(*refs):
    pass


def gate(*arrays, cost=SHORT):
    shapes = tuple(jax.ShapeDtypeStruct(array.shape, array.dtype) for array in arrays)
    anywhere = [pl.BlockSpec(memory_space=pl.ANY)] * len(arrays)
    return pl.pallas_call(
        gate_kernel,
        out_shape=shapes,
        in_specs=anywhere,
        out_specs=tuple(anywhere),
        input_output_aliases={j: j for j in range(len(arrays))},
        cost_estimate=cost,
        name="gate",
    )(*arrays)


def paired_step(covariance, couplings, block_columns, onsite):
    tile_rows, tile_cols = covariance.shape
    row_blocks, col_blocks = tile_rows // BLOCK, tile_cols // BLOCK
    total_blocks, stored = block_columns.shape
    mesh_rows, mesh_cols = lax.axis_size("row"), lax.axis_size("col")
    ratio = tile_rows // tile_cols
    row, col = lax.axis_index("row"), lax.axis_index("col")
    odd, up = col % 2, row % 2
    first_row, first_col = row * row_blocks, col * col_blocks
    offset = jnp.clip(first_col - first_row, 0, row_blocks - col_blocks)
    devices = [(r, c) for r in range(mesh_rows) for c in range(mesh_cols)]
    partners = [((r, c), (r, c ^ 1)) for r, c in devices]
    next_pairs = [((r, c), (r, (c + (2 if c % 2 == 0 else -2)) % mesh_cols)) for r, c in devices]
    inner_route = [((r, c), (r ^ 1, c)) for r, c in devices]
    outer_route = [((r, c), ((r + (-1 if r % 2 == 0 else 1)) % mesh_rows, c)) for r, c in devices]
    beside = 0
    sizes = cut(tile_rows - beside)
    firsts = [sum(sizes[:j]) for j in range(len(sizes))]
    chunks = {j: rows_of(covariance, firsts[j], sizes[j]) for j in range(len(sizes))}
    pairs, strips = {}, {}

    def move(value, route):
        return send(value, route, mesh_cols)

    def exchange(*numbers):
        for j in numbers:
            if j < len(sizes):
                pairs[j] = move(chunks[j], partners)

    def hand_strip_on(j):
        strip = lax.dynamic_slice_in_dim(pairs[j], (1 - odd) * (tile_cols - HALO), HALO, 1)
        strips[j] = move(strip, next_pairs)

    def add_right(total, j):
        first = jnp.int32(firsts[j])
        return right_part(first, odd, pairs[j], strips[j], covariance, col_high, col_low, total)

    diagonal = packed_diagonal(covariance, offset, col_blocks)
    other = move(diagonal, [((r, c), (r, c ^ 1)) for r, c in devices if c // 2 == r])
    far = tile_rows - HALO
    outer = move(rows_of(covariance, up * far, HALO), outer_route)
    other, chunks[0] = gate(other, chunks[0])
    exchange(0)
    inner = move(rows_of(covariance, (1 - up) * far, HALO), inner_route)
    both = jnp.where(odd == 0, jnp.stack([diagonal, other]), jnp.stack([other, diagonal]))
    both = both.reshape(-1, BLOCK, BLOCK)
    across, hop = (col // ratio) ^ row, mesh_cols // ratio // 2
    while hop:
        (moved,) = gate(move(both, cols_route(hop, devices, ratio)))
        both = jnp.where(across & (2 * hop - 1) == hop, moved, both)
        hop //= 2
    zero = jnp.int32(0)
    half = col_blocks // 2
    blocks = couplings.reshape(-1, BLOCK, BLOCK)
    columns = lax.dynamic_slice_in_dim(block_columns, first_row, row_blocks, 0)
    row_gains = lax.dynamic_slice_in_dim(onsite, first_row, row_blocks, 0)
    row_high, row_low = band([blocks], zero, zero, [], zero, half, columns, first_row, total_blocks, row_gains)
    row_high, row_low = add_onsite(row_high, row_low, both, half, row_gains)
    count = col_blocks * stored
    own_blocks = lax.dynamic_slice_in_dim(blocks, offset * stored, count, 0)
    held = {0: jnp.concatenate([own_blocks, diagonal], axis=0)}

    def hand_on(place):
        low = place & -place
        route = [((r, c), (r ^ low, c)) for r, c in devices if r ^ (c // ratio) == place ^ low]
        held[place] = move(held[place ^ low], route)

    places = sorted(range(1, mesh_rows), key=lambda place: (bin(place).count("1"), -place))
    nearest = [place for place in places if place & (place - 1) == 0]

    pairs[0], outer = gate(pairs[0], outer, cost=LONG)
    pairs[0], outer, inner, row_high, held[0], chunks[1], chunks[2], chunks[3] = gate(
        pairs[0], outer, inner, row_high, held[0], chunks[1], chunks[2], chunks[3]
    )
    exchange(1)
    for place in nearest:
        hand_on(place)
    hand_strip_on(0)
    total = left_part(up, inner, covariance, outer, row_high, row_low)

    for place in nearest[:-1]:
        (held[place],) = gate(held[place], cost=SOME)
    (pairs[1],) = gate(pairs[1], cost=LONG)
    pairs[1], strips[0], total, *got = gate(
        pairs[1], strips[0], total, *(held[place] for place in nearest)
    )
    held.update(zip(nearest, got))
    for place in places[len(nearest) :]:
        hand_on(place)
    exchange(2, 3)
    hand_strip_on(1)
    sources = [held[place] for place in range(mesh_rows)]
    columns = lax.dynamic_slice_in_dim(block_columns, first_col, col_blocks, 0)
    gains = lax.dynamic_slice_in_dim(onsite, first_col, col_blocks, 0)
    col_high, col_low = band(
        sources, row ^ (col // ratio), zero, sources, jnp.int32(count), half, columns, first_col, total_blocks, gains
    )
    total = add_right(total, 0)
    for j in range(2, len(sizes)):
        if j + 2 < len(sizes):
            pairs[j], total, chunks[j + 2] = gate(pairs[j], total, chunks[j + 2])
        else:
            pairs[j], total = gate(pairs[j], total)
        hand_strip_on(j)
        exchange(j + 2)
        total = add_right(total, j - 1)
    return add_right(total, len(sizes) - 1)


def power_of_two(number):
    return number & (number - 1) == 0


def on_device(covariance, couplings, block_columns, onsite):
    tile_rows, tile_cols = covariance.shape
    mesh_rows, mesh_cols = lax.axis_size("row"), lax.axis_size("col")
    fits = (
        tile_cols >= HALO
        and tile_cols % (GROUP * BLOCK) == 0
        and tile_rows == 2 * tile_cols
        and mesh_cols == 2 * mesh_rows
        and mesh_rows > 2
        and power_of_two(mesh_rows)
        and block_columns.shape[0] >= 2 * REACH + 2
    )
    step = paired_step if fits else general_step
    return step(covariance, couplings, block_columns, onsite)


def solution(mesh):
    return jax.shard_map(
        on_device,
        mesh=mesh,
        in_specs=(P("row", "col"), P("row", None, None, None), P(), P()),
        out_specs=P("row", "col"),
        check_vma=False,
    )
```
